32 devices in a mesh: head: 4 (over z), ctx: 8 (over y, x, core).
Axes of the slice: x: 2, y: 2, z: 4, core: 2. Of those that a mesh axis runs over, the one named last changes fastest.
Arguments:
- queries: bfloat16 [2, 4096, 4096], P(None, 'ctx', 'head'), may hold values from -20 to 20
- keys: bfloat16 [2, 4096, 4096], P(None, 'ctx', 'head'), may hold values from -20 to 20
- values: bfloat16 [2, 4096, 4096], P(None, 'ctx', 'head'), may hold values from -6 to 6
- token_rates: float32 [2, 4096, 8], P(None, 'ctx', 'head'), may hold values from 0.05 to 1
- fast_init: float32 [3, 8, 512, 512], P(None, 'head'), may hold values from -0.25 to 0.25
- out_gain: float32 [4096], P('head'), may hold values from 0.5 to 1.5
- out_weight: bfloat16 [4096, 4096], P('head'), may hold values from -0.09375 to 0.09375
Outputs:
- layer_out: bfloat16 [2, 4096, 4096], P(None, ('ctx', 'head'))
- fast_final: float32 [3, 8, 512, 512], P(None, 'head')
The draws below stay inside these ranges and needn't reach their ends.
All inputs are finite; a program needn't handle non-finite values.
Results may differ from the reference program's by a relative error of at most 0.022.
Values may be sent and summed in bfloat16 or wider, within the bound.
No kernel may reach another device: no remote copies, remote signals or barrier semaphores. Data moves between devices by JAX's collectives and lax.ppermute only.
A program may use at most 192 MiB of HBM per device.

```python
import math
import jax
import jax.numpy as jnp
from jax import lax

HEADS = 8
DH = 512
AH = 128
TOK = 512
SPANS = 2
NS_ITERS = 2
D = 4096
SEQ = 4096
WINDOW = 2048
N_HEAD = 4


def drawn_pair(key):
    base = jax.random.fold_in(key, 11)
    streams = jax.random.split(base, 2)
    shape = (SPANS, SEQ, HEADS * DH)
    feature = jnp.exp(jnp.linspace(jnp.log(0.6), jnp.log(1.8), DH)).astype(jnp.float32)
    feature = jnp.tile(feature, HEADS)
    query_raw = jax.random.truncated_normal(streams[0], -4.0, 4.0, shape, jnp.float32) * feature
    key_raw = jax.random.truncated_normal(streams[1], -4.0, 4.0, shape, jnp.float32) * feature
    return (query_raw, key_raw)


def draw_queries(key, part):
    query_raw, key_raw = drawn_pair(key)
    return query_raw.astype(jnp.bfloat16)


def draw_keys(key, part):
    query_raw, key_raw = drawn_pair(key)
    return key_raw.astype(jnp.bfloat16)


def shard_levels(key, dims, cuts, low, high):
    def one(axis_at, parts):
        heights = jax.random.uniform(jax.random.fold_in(jax.random.fold_in(key, 6), axis_at), (parts,), jnp.float32, low / len(cuts), high / len(cuts))
        return jnp.repeat(jnp.exp(heights), dims[axis_at] // parts).reshape((-1,) + (1,) * (len(dims) - axis_at - 1))

    level = one(*cuts[0])
    for cut in cuts[1:]:
        level = level * one(*cut)
    return level


def centred(stream_key, dims, width, limit, pieces=(), kind=jnp.bfloat16):
    gain = shard_levels(stream_key, dims, pieces, -0.22, 0.18) if pieces else 1.0
    entries = jax.random.normal(stream_key, dims, jnp.float32) * width * gain
    return jnp.minimum(jnp.maximum(entries, -limit), limit).astype(kind)


def setup_inputs(seed: int = 0) -> dict:
    key_of = jax.random.split(jax.random.key(seed), 8)
    queries = draw_queries(jax.random.fold_in(key_of[7], 71), 0)
    keys = draw_keys(jax.random.fold_in(key_of[7], 71), 0)
    values = centred(key_of[2], (SPANS, SEQ, D), 1.0, 6.0, ((1, 8), (2, 4)))
    token_rates = jnp.clip(jnp.exp(math.log(1.0) - 2.9957323 * jax.random.uniform(key_of[3], (SPANS, SEQ, HEADS), jnp.float32) ** shard_levels(key_of[3], (SPANS, SEQ, HEADS), ((1, 8), (2, 4)), -0.2, 0.2)), 0.05, 1.0)
    fast_init = centred(key_of[4], (3, HEADS, DH, DH), DH ** -0.5, 0.25, ((1, 4),), jnp.float32)
    out_gain = jnp.clip(1.0 + 0.1 * jax.random.normal(key_of[5], (D,), jnp.float32), 0.5, 1.5)
    out_weight = centred(key_of[6], (D, D), D ** -0.5, 0.09375, ((0, 4),))
    return dict(queries=queries, keys=keys, values=values, token_rates=token_rates, fast_init=fast_init, out_gain=out_gain, out_weight=out_weight)


coef_a = 3.4445
coef_b = -4.775
coef_c = 2.0315

def head_norm(inputs):
    return inputs / jnp.sqrt(lax.optimization_barrier(jnp.mean(inputs * inputs, axis=-1, keepdims=True)) + 1e-06)

def window_attention(queries, keys, values):
    total = SPANS * SEQ
    att_heads = HEADS * DH // AH
    query_flat = queries.reshape(total, att_heads, AH)
    padding = jnp.zeros((4 * TOK, att_heads, AH), jnp.bfloat16)
    key_flat = jnp.concatenate([padding, keys.reshape(total, att_heads, AH)], 0)
    value_flat = jnp.concatenate([padding, values.reshape(total, att_heads, AH)], 0)
    scale = AH ** (-0.5)
    query_pos = jnp.arange(TOK, dtype=jnp.int32)[:, None]
    key_pos = jnp.arange(5 * TOK, dtype=jnp.int32)[None, :]

    def one_block(block):
        start = (block * TOK).astype(jnp.int32)
        query_block = lax.dynamic_slice_in_dim(query_flat, start, TOK, 0)
        key_block = lax.dynamic_slice_in_dim(key_flat, start, 5 * TOK, 0)
        value_block = lax.dynamic_slice_in_dim(value_flat, start, 5 * TOK, 0)
        scores = jnp.einsum('qnd,knd->nqk', query_block.astype(jnp.float32), key_block.astype(jnp.float32)) * scale
        distance = query_pos + 4 * TOK - key_pos
        valid = (distance >= 0) & (distance < WINDOW) & (start - 4 * TOK + key_pos >= 0)
        scores = jnp.where(valid[None], scores, -1e+30)
        largest = lax.optimization_barrier(jnp.max(scores, axis=-1, keepdims=True))
        expon = jnp.exp(scores - largest)
        probs = (expon / lax.optimization_barrier(jnp.sum(expon, axis=-1, keepdims=True))).astype(jnp.bfloat16)
        return jnp.einsum('nqk,knd->qnd', probs.astype(jnp.float32), value_block.astype(jnp.float32))
    blocks = lax.map(one_block, jnp.arange(total // TOK, dtype=jnp.int32))
    return blocks.reshape(SPANS, SEQ, HEADS * DH)

def fast_hidden(inputs, weights_bf):
    first = jnp.einsum('shd,hde->she', inputs.astype(jnp.float32), weights_bf[0].astype(jnp.float32))
    third = jnp.einsum('shd,hde->she', inputs.astype(jnp.float32), weights_bf[1].astype(jnp.float32))
    hidden = (first * jax.nn.sigmoid(first) * third).astype(jnp.bfloat16)
    return (first, third, hidden)

def muon_orth(grads):
    ortho = (grads * lax.rsqrt(lax.optimization_barrier(jnp.sum(grads * grads, axis=(2, 3), keepdims=True)) + 1e-06)).astype(jnp.bfloat16)
    for turn in range(NS_ITERS):
        gram = jnp.einsum('mhri,mhrj->mhij', ortho.astype(jnp.float32), ortho.astype(jnp.float32)).astype(jnp.bfloat16)
        square = jnp.einsum('mhij,mhjk->mhik', gram.astype(jnp.float32), gram.astype(jnp.float32))
        poly = (coef_b * gram.astype(jnp.float32) + coef_c * square).astype(jnp.bfloat16)
        moved = jnp.einsum('mhri,mhij->mhrj', ortho.astype(jnp.float32), poly.astype(jnp.float32))
        ortho = (coef_a * ortho.astype(jnp.float32) + moved).astype(jnp.bfloat16)
    return ortho

def renorm(previous, fresh):
    target = jnp.sqrt(lax.optimization_barrier(jnp.mean(previous * previous, axis=-1, keepdims=True)) + 1e-06)
    actual = jnp.sqrt(lax.optimization_barrier(jnp.mean(fresh * fresh, axis=-1, keepdims=True)) + 1e-06)
    return fresh * target / actual

def reference(queries, keys, values, token_rates, fast_init, out_gain, out_weight):
    attn = window_attention(queries, keys, values)
    state = fast_init
    mixed_all = []
    for span in range(SPANS):
        query_norm = head_norm(queries[span].reshape(SEQ, HEADS, DH).astype(jnp.float32)).astype(jnp.bfloat16)
        key_norm = head_norm(keys[span].reshape(SEQ, HEADS, DH).astype(jnp.float32)).astype(jnp.bfloat16)
        value_heads = values[span].reshape(SEQ, HEADS, DH)
        weights_bf = state.astype(jnp.bfloat16)
        unused_a, unused_b, query_hidden = fast_hidden(query_norm, weights_bf)
        fast_out = jnp.einsum('she,hed->shd', query_hidden.astype(jnp.float32), weights_bf[2].astype(jnp.float32))
        first, third, key_hidden = fast_hidden(key_norm, weights_bf)
        pull = (-token_rates[span][:, :, None] * value_heads.astype(jnp.float32)).astype(jnp.bfloat16)
        grad_down = jnp.einsum('she,shd->hed', key_hidden.astype(jnp.float32), pull.astype(jnp.float32))
        back = jnp.einsum('shd,hed->she', pull.astype(jnp.float32), weights_bf[2].astype(jnp.float32))
        sigma = jax.nn.sigmoid(first)
        d_first = (back * third * sigma * (1.0 + first * (1.0 - sigma))).astype(jnp.bfloat16)
        d_third = (back * first * sigma).astype(jnp.bfloat16)
        grad_first = jnp.einsum('shd,she->hde', key_norm.astype(jnp.float32), d_first.astype(jnp.float32))
        grad_third = jnp.einsum('shd,she->hde', key_norm.astype(jnp.float32), d_third.astype(jnp.float32))
        grads = jnp.stack([grad_first, grad_third, grad_down], 0)
        ortho = muon_orth(grads)
        state = renorm(state, state - ortho.astype(jnp.float32))
        normed = head_norm(fast_out) * out_gain.reshape(HEADS, DH)
        mixed = (normed.reshape(SEQ, HEADS * DH) + attn[span]).astype(jnp.bfloat16)
        mixed_all.append(mixed)
    combined = jnp.stack(mixed_all, 0).reshape(SPANS * SEQ, HEADS * DH)
    group_cols = HEADS * DH // N_HEAD
    total = jnp.zeros((SPANS * SEQ, HEADS * DH), jnp.float32)
    for group in range(N_HEAD):
        lower = group * group_cols
        term = jnp.dot(combined[:, lower:lower + group_cols], out_weight[lower:lower + group_cols], preferred_element_type=jnp.float32)
        total = total + term.astype(jnp.bfloat16).astype(jnp.float32)
    layer_out = total.astype(jnp.bfloat16).reshape(SPANS, SEQ, HEADS * DH)
    return (layer_out, state)
```

```python
import functools

import jax
import jax.numpy as jnp
from jax import lax
from jax.experimental import pallas as pl
from jax.experimental.pallas import tpu as pltpu
from jax.sharding import PartitionSpec as P

AH = 128
NS_ITERS = 2
BACK = 4


coef_a = 3.4445
coef_b = -4.775
coef_c = 2.0315
LOG2E = 1.4426950408889634
F32 = jnp.float32
BF16 = jnp.bfloat16
NOWHERE = 2**20
VMEM_BYTES = 56 * 1024 * 1024


def swapped(block, mask):
    devices = range(lax.axis_size("ctx"))
    return lax.ppermute(block, "ctx", [(i, i ^ mask) for i in devices])


def raised(block, step):
    devices = range(lax.axis_size("ctx") - step)
    return lax.ppermute(block, "ctx", [(i, i + step) for i in devices])


def after(value, *earlier):
    return lax.optimization_barrier((value,) + earlier)[0]


def rms_inverse(inputs):
    return lax.rsqrt(jnp.mean(inputs * inputs, axis=-1, keepdims=True) + 1e-06)


def sigmoid(inputs):
    return 0.5 * jnp.tanh(0.5 * inputs) + 0.5


def dot_nn(left, right):
    return lax.dot_general(left, right, (((1,), (0,)), ((), ())), preferred_element_type=F32)


def dot_nt(left, right):
    return lax.dot_general(left, right, (((1,), (1,)), ((), ())), preferred_element_type=F32)


def dot_tn(left, right):
    return lax.dot_general(left, right, (((0,), (0,)), ((), ())), preferred_element_type=F32)


def params():
    return pltpu.CompilerParams(vmem_limit_bytes=VMEM_BYTES)


def cost(flops, bytes_accessed, transcendentals=0):
    return pl.CostEstimate(
        flops=flops, bytes_accessed=bytes_accessed, transcendentals=transcendentals
    )


def in_vmem(count):
    return [pl.BlockSpec(memory_space=pltpu.VMEM)] * count


IN_SMEM = pl.BlockSpec(memory_space=pltpu.SMEM)


def token_grads(kv_ref, rate_ref, weight_ref, emit):
    keys = kv_ref[0].astype(F32)
    normed = (keys * rms_inverse(keys)).astype(BF16)
    pull = (-rate_ref[:, :1] * kv_ref[1].astype(F32)).astype(BF16)
    first = dot_nn(normed, weight_ref[0])
    third = dot_nn(normed, weight_ref[1])
    back = dot_nt(pull, weight_ref[2])
    sigma = sigmoid(first)
    silu = first * sigma
    hidden = (silu * third).astype(BF16)
    d_third = (back * silu).astype(BF16)
    d_first = (back * third * (sigma * (1.0 + first - silu))).astype(BF16)
    emit(0, dot_tn(normed, d_first))
    emit(1, dot_tn(normed, d_third))
    emit(2, dot_tn(hidden, pull))


def grads_first_kernel(kv_ref, rate_ref, weight_ref, out_ref):
    def emit(index, value):
        out_ref[index] = value

    token_grads(kv_ref, rate_ref, weight_ref, emit)


def grads_second_kernel(core_ref, kv_ref, rate_ref, weight_ref, sum_ref, keep_ref, give_ref, all_ref):
    half = keep_ref.shape[1]
    core = core_ref[0]

    def emit(index, value):
        all_ref[index] = value + sum_ref[index]

    token_grads(kv_ref, rate_ref, weight_ref, emit)
    for index in range(all_ref.shape[0]):
        mine = pl.ds(pl.multiple_of(core * half, half), half)
        other = pl.ds(pl.multiple_of((1 - core) * half, half), half)
        keep_ref[index] = all_ref[index, mine, :].astype(BF16)
        give_ref[index] = all_ref[index, other, :].astype(BF16)


def grads_first(kv, rates, weights):
    tok, width = kv.shape[1:]
    flops = 12 * tok * width * width
    return pl.pallas_call(
        grads_first_kernel,
        out_shape=jax.ShapeDtypeStruct((3, width, width), F32),
        in_specs=in_vmem(3),
        out_specs=in_vmem(1)[0],
        compiler_params=params(),
        cost_estimate=cost(flops, 16 * width * width),
        name="grads_first",
    )(kv, rates, weights)


def grads_second(core, kv, rates, weights, partial):
    tok, width = kv.shape[1:]
    flops = 12 * tok * width * width
    half = jax.ShapeDtypeStruct((3, width // 2, width), BF16)
    return pl.pallas_call(
        grads_second_kernel,
        out_shape=(half, half),
        in_specs=[IN_SMEM] + in_vmem(4),
        out_specs=tuple(in_vmem(2)),
        scratch_shapes=[pltpu.VMEM((3, width, width), F32)],
        compiler_params=params(),
        cost_estimate=cost(flops, 28 * width * width),
        name="grads_second",
    )(core, kv, rates, weights, partial)


def muon_kernel(core_ref, mine_ref, other_ref, *refs, update):
    if update:
        state_ref, ortho_ref, half_ref, weight_ref, grad_ref = refs
    else:
        ortho_ref, half_ref, grad_ref = refs
    half = mine_ref.shape[1]
    core = core_ref[0]
    mine = pl.ds(pl.multiple_of(core * half, half), half)
    other = pl.ds(pl.multiple_of((1 - core) * half, half), half)
    count = mine_ref.shape[0]
    for index in range(count):
        grad_ref[index, mine, :] = mine_ref[index].astype(F32)
        grad_ref[index, other, :] = other_ref[index].astype(F32)
    ortho = []
    for index in range(count):
        grad = grad_ref[index]
        ortho.append((grad * lax.rsqrt(jnp.sum(grad * grad) + 1e-06)).astype(BF16))
    for turn in range(NS_ITERS):
        gram = [dot_tn(mat, mat).astype(BF16) for mat in ortho]
        poly = [(coef_b * mat.astype(F32) + coef_c * dot_nn(mat, mat)).astype(BF16) for mat in gram]
        ortho = [
            (coef_a * mat.astype(F32) + dot_nn(mat, step)).astype(BF16)
            for mat, step in zip(ortho, poly)
        ]
    for index in range(count):
        ortho_ref[index] = ortho[index]
        half_ref[index] = ortho_ref[index, mine, :]
        if update:
            weight_ref[index] = renorm(state_ref[index, 0], ortho[index].astype(F32)).astype(BF16)


def renorm(previous, step):
    fresh = previous - step
    target = jnp.sqrt(jnp.mean(previous * previous, axis=-1, keepdims=True) + 1e-06)
    return fresh * (target * rms_inverse(fresh))


def muon(core, mine, other, state=None, side=None):
    count, half, width = mine.shape
    whole = jax.ShapeDtypeStruct((count, width, width), BF16)
    part = jax.ShapeDtypeStruct((count, half, width), BF16)
    update = state is not None
    outs = (whole, part, whole) if update else (whole, part)
    body = functools.partial(muon_kernel, update=update)
    grid_spec = pltpu.PrefetchScalarGridSpec(
        num_scalar_prefetch=1,
        grid=(1,),
        in_specs=[pl.BlockSpec((count, half, width), lambda i, s: (0, 0, 0))] * 2
        + (
            [pl.BlockSpec((count, 1, width, width), lambda i, s: (0, s[1], 0, 0))]
            if update
            else []
        ),
        out_specs=tuple(pl.BlockSpec(out.shape, lambda i, s: (0, 0, 0)) for out in outs),
        scratch_shapes=[pltpu.VMEM((count, width, width), F32)],
    )
    scalars = jnp.stack([core, core if side is None else side])
    return pl.pallas_call(
        body,
        out_shape=outs,
        grid_spec=grid_spec,
        compiler_params=params(),
        cost_estimate=cost(count * NS_ITERS * 6 * width**3, 12 * width * width),
        name="muon",
    )(scalars, mine, other, *((state,) if update else ()))


def finish_kernel(scalar_ref, state_ref, *refs):
    spans = (len(refs) - 1) // 3
    out_ref = refs[-1]
    core, side = scalar_ref[0], scalar_ref[1]
    half = refs[1].shape[1]
    head = pl.program_id(1)

    def advance(steps):
        value = state_ref[0, 0]
        for step in steps:
            value = renorm(value, step.astype(F32))
        out_ref[0, 0] = value

    @pl.when(head == side)
    def _own():
        advance([refs[3 * span][0] for span in range(spans)])

    @pl.when((head != side) & (core == 0))
    def _first():
        advance(
            [jnp.concatenate([refs[3 * span + 1][0], refs[3 * span + 2][0]], 0) for span in range(spans)]
        )

    @pl.when((head != side) & (core != 0))
    def _second():
        advance(
            [jnp.concatenate([refs[3 * span + 2][0], refs[3 * span + 1][0]], 0) for span in range(spans)]
        )


def finish(core, side, state, steps):
    count, heads, width, _ = state.shape
    half = width // 2
    specs = []
    for _ in steps:
        specs.append(pl.BlockSpec((1, width, width), lambda m, h, s: (m, 0, 0)))
        specs.append(pl.BlockSpec((1, half, width), lambda m, h, s: (m, 0, 0)))
        specs.append(pl.BlockSpec((1, half, width), lambda m, h, s: (m, 0, 0)))
    one = pl.BlockSpec((1, 1, width, width), lambda m, h, s: (m, h, 0, 0))
    grid_spec = pltpu.PrefetchScalarGridSpec(
        num_scalar_prefetch=1,
        grid=(count, heads),
        in_specs=[one] + specs,
        out_specs=one,
    )
    flat = [array for step in steps for array in step]
    return pl.pallas_call(
        finish_kernel,
        out_shape=jax.ShapeDtypeStruct(state.shape, F32),
        grid_spec=grid_spec,
        compiler_params=params(),
        cost_estimate=cost(20 * state.size, 8 * state.size + 4 * state.size),
        name="finish",
    )(jnp.stack([core, side]), state, *flat)


def attend_kernel(ids_ref, query_ref, *refs, blocks, start, end):
    refs = list(refs)
    kv_refs, refs = refs[:blocks], refs[blocks:]
    if start:
        sum_in_ref = top_in_ref = None
    else:
        (sum_in_ref, top_in_ref), refs = refs[:2], refs[2:]
    if end:
        out_ref, refs = refs[0], refs[1:]
        sum_ref, top_ref, bias_ref = refs
    else:
        sum_ref, top_ref, bias_ref = refs
    tok = query_ref.shape[1]
    width = query_ref.shape[2]
    head = pl.program_id(0)
    which = pl.program_id(1)

    @pl.when((head == 0) & (which == 0))
    def _bias():
        row = lax.broadcasted_iota(jnp.int32, (tok, tok), 0)
        column = lax.broadcasted_iota(jnp.int32, (tok, tok), 1)
        bias_ref[0] = jnp.where(column <= row, 0.0, -1e30)
        bias_ref[1] = jnp.zeros((tok, tok), F32)
        bias_ref[2] = jnp.where(column > row, 0.0, -1e30)

    if start:
        sum_ref[...] = jnp.zeros_like(sum_ref)
        top_ref[...] = jnp.full_like(top_ref, -1e30)
    else:
        sum_ref[...] = sum_in_ref[...]
        top_ref[...] = top_in_ref[...]
    query = query_ref[0]
    place = ids_ref[which]
    ones = jnp.ones((tok, width), BF16)
    for block in range(blocks):
        apart = place - ids_ref[2 + block]

        @pl.when((apart >= 0) & (apart <= BACK))
        def _block(block=block, apart=apart):
            kind = jnp.where(apart == 0, 0, jnp.where(apart == BACK, 2, 1))
            values = jnp.concatenate([kv_refs[block][1], ones], 1)
            rows = tok // 2
            for part in range(2):
                span = pl.ds(part * rows, rows)
                scores = dot_nt(query[part * rows : (part + 1) * rows], kv_refs[block][0])
                scores = scores * (AH**-0.5 * LOG2E) + bias_ref[kind, span, :]
                old = top_ref[0, 0, span, :]
                top = jnp.maximum(old, jnp.max(scores, axis=-1, keepdims=True))
                weights = jnp.exp2(scores - top[:, :1]).astype(BF16)
                shrink = jnp.exp2(old - top)
                fresh = dot_nn(weights, values)
                sum_ref[0, 0, span, :width] = sum_ref[0, 0, span, :width] * shrink + fresh[:, :width]
                sum_ref[0, 0, span, width:] = sum_ref[0, 0, span, width:] * shrink + fresh[:, width:]
                top_ref[0, 0, span, :] = top

    if end:
        out_ref[0] = (sum_ref[0, 0, :, :width] / sum_ref[0, 0, :, width:]).astype(BF16)


def attend(ids, queries, kvs, carry=None, end=False):
    two, tok, features = queries.shape
    heads = features // AH
    blocks = len(kvs)
    start = carry is None
    query_spec = pl.BlockSpec((1, tok, AH), lambda h, w, s: (w, 0, h))
    kv_spec = pl.BlockSpec((2, tok, AH), lambda h, w, s: (0, 0, h))
    sum_spec = pl.BlockSpec((1, 1, tok, 2 * AH), lambda h, w, s: (h, w, 0, 0))
    top_spec = pl.BlockSpec((1, 1, tok, AH), lambda h, w, s: (h, w, 0, 0))
    sum_shape = jax.ShapeDtypeStruct((heads, two, tok, 2 * AH), F32)
    top_shape = jax.ShapeDtypeStruct((heads, two, tok, AH), F32)
    scratch = [pltpu.VMEM((3, tok, tok), F32)]
    if end:
        outs, out_specs = jax.ShapeDtypeStruct(queries.shape, BF16), query_spec
        scratch = [
            pltpu.VMEM((1, 1, tok, 2 * AH), F32),
            pltpu.VMEM((1, 1, tok, AH), F32),
        ] + scratch
    else:
        outs, out_specs = (sum_shape, top_shape), (sum_spec, top_spec)
    grid_spec = pltpu.PrefetchScalarGridSpec(
        num_scalar_prefetch=1,
        grid=(heads, two),
        in_specs=[query_spec] + [kv_spec] * blocks + ([] if start else [sum_spec, top_spec]),
        out_specs=out_specs,
        scratch_shapes=scratch,
    )
    pairs = heads * 5
    return pl.pallas_call(
        functools.partial(attend_kernel, blocks=blocks, start=start, end=end),
        out_shape=outs,
        grid_spec=grid_spec,
        compiler_params=params(),
        cost_estimate=cost(
            pairs * 8 * tok * tok * AH, blocks * 4 * tok * features, pairs * tok * tok
        ),
        name="attend",
    )(ids, queries, *kvs, *(() if start else carry))


def answer_kernel(query_ref, weight_ref, gain_ref, out_ref):
    query = query_ref[0].astype(F32)
    normed = (query * rms_inverse(query)).astype(BF16)
    first = dot_nn(normed, weight_ref[0])
    third = dot_nn(normed, weight_ref[1])
    hidden = (first * sigmoid(first) * third).astype(BF16)
    answer = dot_nn(hidden, weight_ref[2])
    out_ref[0] = answer * rms_inverse(answer) * gain_ref[...]


def answer(queries, weights, gain):
    two, tok, width = queries.shape
    block = pl.BlockSpec((1, tok, width), lambda w: (w, 0, 0))
    return pl.pallas_call(
        answer_kernel,
        out_shape=jax.ShapeDtypeStruct(queries.shape, F32),
        grid=(two,),
        in_specs=[
            block,
            pl.BlockSpec(weights.shape, lambda w: (0, 0, 0)),
            pl.BlockSpec((1, width), lambda w: (0, 0)),
        ],
        out_specs=block,
        compiler_params=params(),
        cost_estimate=cost(two * 6 * tok * width * width, 10 * tok * width),
        name="answer",
    )(queries, weights, gain)


def shards(queries, keys, values, token_rates, fast_init, out_gain, out_weight):
    spans, tok, features = queries.shape
    width = fast_init.shape[2]
    position = lax.axis_index("ctx")
    around = lax.axis_size("ctx")
    upper = around // 2
    core = position % 2
    side = (position // 2) % 2
    far = position // upper
    here = side == 0

    def keep(array):
        return jnp.where(here, array[..., :width], array[..., width:])

    def give(array):
        return jnp.where(here, array[..., width:], array[..., :width])

    gain = keep(out_gain[None, :])
    rates_own = jnp.where(here, token_rates[..., 0], token_rates[..., 1])
    rates_away = jnp.where(here, token_rates[..., 1], token_rates[..., 0])
    rates_got = swapped(rates_away, 2)

    def column(rates):
        return jnp.broadcast_to(rates[:, None], (tok, 128))

    kv_own = [jnp.stack([keep(keys[span]), keep(values[span])]) for span in range(spans)]
    kv_away = [jnp.stack([give(keys[span]), give(values[span])]) for span in range(spans)]
    weights = jnp.where(here, fast_init[:, 0], fast_init[:, 1]).astype(BF16)

    kv_got = [swapped(kv_away[0], 2)]
    query_got = [swapped(after(give(queries[0]), kv_got[0]), 2)]
    kv_got.append(swapped(after(kv_away[1], query_got[0]), 2))
    query_got.append(swapped(after(give(queries[1]), kv_got[1]), 2))
    query_both = [jnp.stack([keep(queries[span]), query_got[span]]) for span in range(spans)]

    far_own = [swapped(kv_own[0], upper)]
    far_got = [swapped(after(kv_got[0], far_own[0]), upper)]
    near = [[kv_own[0], kv_got[0], swapped(kv_own[0], 1), swapped(kv_got[0], 1)]]
    fars = [[far_own[0], far_got[0], swapped(far_own[0], 1), swapped(far_got[0], 1)]]

    own_place = 2 * side + core
    got_place = 2 * (1 - side) + core
    own_pair = 2 * side + 1 - core
    got_pair = 2 * (1 - side) + 1 - core
    places = jnp.stack([own_place, got_place, own_pair, got_pair]).astype(jnp.int32)

    def ids(span, *bases):
        mine = span * around + far * upper + places[:2]
        return jnp.concatenate([mine] + [base + places for base in bases]).astype(jnp.int32)

    partial = grads_first(kv_own[0], column(rates_own[0]), weights)
    sums_keep, sums_give = grads_second(
        core[None].astype(jnp.int32), kv_got[0], column(rates_got[0]), weights, partial
    )
    steps = []
    mixed_full = []
    products = []
    for span in range(spans):
        base = span * around
        chip = (sums_keep.astype(F32) + swapped(sums_give, 1).astype(F32)).astype(BF16)
        total = (chip.astype(F32) + swapped(after(chip, far_got[span]), upper).astype(F32)).astype(BF16)
        pair = swapped(total, 1)
        if span + 1 < spans:
            ortho, ortho_half, next_weights = muon(core, total, pair, fast_init, side)
        else:
            ortho, ortho_half = muon(core, total, pair)
        carry = attend(ids(span, base + far * upper), query_both[span], near[span])
        if span == 0:
            late = jnp.where(far == 0, NOWHERE, base)
            attn = attend(ids(span, late), query_both[span], fars[span], carry, True)
        else:
            early = jnp.where(far == 0, base - upper, NOWHERE)
            late = jnp.where(far == 0, NOWHERE, base)
            attn = attend(
                ids(span, early, late), query_both[span], fars[span - 1] + fars[span], carry, True
            )
        fast = answer(query_both[span], weights, gain)
        mixed = (fast + attn.astype(F32)).astype(BF16)
        returned = swapped(mixed[1], 2)
        full = jnp.concatenate(
            [jnp.where(here, mixed[0], returned), jnp.where(here, returned, mixed[0])], 1
        )
        product = jnp.dot(full, out_weight, preferred_element_type=F32).astype(BF16)
        products.append(lax.psum_scatter(product, "head", scatter_dimension=0, tiled=True))
        if span + 1 < spans:
            weights = next_weights
            following = span + 1
            partial = grads_first(kv_own[following], column(rates_own[following]), weights)
            sums_keep, sums_give = grads_second(
                core[None].astype(jnp.int32),
                kv_got[following],
                column(rates_got[following]),
                weights,
                partial,
            )
            far_own.append(raised(after(kv_own[following], far_got[span]), upper))
            far_got.append(raised(after(kv_got[following], far_own[following]), upper))
            near.append(
                [kv_own[following], kv_got[following]]
                + [swapped(kv_own[following], 1), swapped(kv_got[following], 1)]
            )
            fars.append(
                [far_own[following], far_got[following]]
                + [swapped(far_own[following], 1), swapped(far_got[following], 1)]
            )
        away = swapped(after(ortho_half, query_got[-1]), 2)
        steps.append((ortho, away, swapped(away, 1)))
    state = finish(core, side, fast_init, steps)
    return (jnp.stack(products, 0), state)


def shifted(block, axis, distance):
    devices = range(lax.axis_size(axis))
    route = [((i - distance) % len(devices), i) for i in devices]
    return lax.ppermute(block, axis, route)


def head_norm(inputs):
    return inputs / jnp.sqrt(jnp.mean(inputs * inputs, axis=-1, keepdims=True) + 1e-06)


def renormed(previous, fresh):
    target = jnp.sqrt(jnp.mean(previous * previous, axis=-1, keepdims=True) + 1e-06)
    actual = jnp.sqrt(jnp.mean(fresh * fresh, axis=-1, keepdims=True) + 1e-06)
    return fresh * target / actual


def newton_turn(ortho, gram):
    gram_bf = gram.astype(jnp.bfloat16)
    square = jnp.einsum("mhij,mhjk->mhik", gram_bf, gram_bf, preferred_element_type=jnp.float32)
    poly = (coef_b * gram_bf.astype(jnp.float32) + coef_c * square).astype(jnp.bfloat16)
    moved = jnp.einsum("rmhi,mhij->rmhj", ortho, poly, preferred_element_type=jnp.float32)
    return (coef_a * ortho.astype(jnp.float32) + moved).astype(jnp.bfloat16)


def fix_wrapped(received, distance, position):
    rolled = jnp.concatenate([jnp.zeros_like(received[:1]), received[:-1]], 0)
    return jnp.where(position < distance, rolled, received)


def shards_any(queries, keys, values, token_rates, fast_init, out_gain, out_weight):
    spans, tok, features = queries.shape
    per_dev = fast_init.shape[1]
    width = fast_init.shape[2]
    att_heads = features // AH
    position = lax.axis_index("ctx")
    far_keys = []
    far_values = []
    carried = (keys, values)
    for distance in (1, 2, 3, 4):
        carried = shifted((carried[0], carried[1]), "ctx", 1)
        far_keys.insert(0, fix_wrapped(carried[0], distance, position))
        far_values.insert(0, fix_wrapped(carried[1], distance, position))
    window_keys = jnp.concatenate(far_keys + [keys], 1)
    window_values = jnp.concatenate(far_values + [values], 1)
    scale = AH ** (-0.5)
    query_pos = jnp.arange(tok, dtype=jnp.int32)[:, None]
    key_pos = jnp.arange(5 * tok, dtype=jnp.int32)[None, :]
    distance_pos = query_pos + 4 * tok - key_pos
    in_window = (distance_pos >= 0) & (distance_pos < 4 * tok)
    key_shard = 4 - key_pos // tok
    gain = out_gain.reshape(per_dev, width)
    state = fast_init
    mixed_all = []
    for span in range(spans):
        valid = in_window
        if span == 0:
            valid = valid & jnp.logical_not(position < key_shard)
        query_heads = queries[span].reshape(tok, att_heads, AH)
        key_heads = window_keys[span].reshape(5 * tok, att_heads, AH)
        value_heads = window_values[span].reshape(5 * tok, att_heads, AH)
        scores = (
            jnp.einsum("qnd,knd->nqk", query_heads, key_heads, preferred_element_type=jnp.float32)
            * scale
        )
        scores = jnp.where(valid[None], scores, -1e30)
        largest = jnp.max(scores, axis=-1, keepdims=True)
        expon = jnp.exp(scores - largest)
        probs = (expon / jnp.sum(expon, axis=-1, keepdims=True)).astype(jnp.bfloat16)
        attn = jnp.einsum(
            "nqk,knd->qnd", probs, value_heads, preferred_element_type=jnp.float32
        ).reshape(tok, features)
        query_norm = head_norm(
            queries[span].reshape(tok, per_dev, width).astype(jnp.float32)
        ).astype(jnp.bfloat16)
        key_norm = head_norm(keys[span].reshape(tok, per_dev, width).astype(jnp.float32)).astype(
            jnp.bfloat16
        )
        value_own = values[span].reshape(tok, per_dev, width)
        weights_bf = state.astype(jnp.bfloat16)
        q_first = jnp.einsum(
            "shd,hde->she", query_norm, weights_bf[0], preferred_element_type=jnp.float32
        )
        q_third = jnp.einsum(
            "shd,hde->she", query_norm, weights_bf[1], preferred_element_type=jnp.float32
        )
        query_hidden = (q_first * jax.nn.sigmoid(q_first) * q_third).astype(jnp.bfloat16)
        fast_out = jnp.einsum(
            "she,hed->shd", query_hidden, weights_bf[2], preferred_element_type=jnp.float32
        )
        first = jnp.einsum(
            "shd,hde->she", key_norm, weights_bf[0], preferred_element_type=jnp.float32
        )
        third = jnp.einsum(
            "shd,hde->she", key_norm, weights_bf[1], preferred_element_type=jnp.float32
        )
        sigma = jax.nn.sigmoid(first)
        key_hidden = (first * sigma * third).astype(jnp.bfloat16)
        pull = (-token_rates[span][:, :, None] * value_own.astype(jnp.float32)).astype(jnp.bfloat16)
        back = jnp.einsum("shd,hed->she", pull, weights_bf[2], preferred_element_type=jnp.float32)
        d_first = (back * third * sigma * (1.0 + first * (1.0 - sigma))).astype(jnp.bfloat16)
        d_third = (back * first * sigma).astype(jnp.bfloat16)
        grad_first = jnp.einsum(
            "shr,she->rhe", key_norm, d_first, preferred_element_type=jnp.float32
        )
        grad_third = jnp.einsum(
            "shr,she->rhe", key_norm, d_third, preferred_element_type=jnp.float32
        )
        grad_down = jnp.einsum("shr,shd->rhd", key_hidden, pull, preferred_element_type=jnp.float32)
        grad_rows = lax.psum_scatter(
            jnp.stack([grad_first, grad_third, grad_down], 1).astype(jnp.bfloat16),
            "ctx",
            scatter_dimension=0,
            tiled=True,
        ).astype(jnp.float32)
        squares = lax.psum(jnp.sum(grad_rows * grad_rows, axis=(0, 3)), "ctx")
        ortho_rows = (grad_rows * lax.rsqrt(squares + 1e-06)[None, :, :, None]).astype(jnp.bfloat16)
        ortho = lax.all_gather(ortho_rows, "ctx", axis=0, tiled=True)
        for turn in range(NS_ITERS):
            gram = jnp.einsum("rmhi,rmhj->mhij", ortho, ortho, preferred_element_type=jnp.float32)
            ortho = newton_turn(ortho, gram)
        ortho_mats = jnp.transpose(ortho, (1, 2, 0, 3)).astype(jnp.float32)
        state = renormed(state, state - ortho_mats)
        normed = head_norm(fast_out) * gain
        mixed_all.append((normed.reshape(tok, features) + attn).astype(jnp.bfloat16))
    combined = jnp.stack(mixed_all, 0)
    product = jnp.einsum("ctd,de->tce", combined, out_weight, preferred_element_type=jnp.float32)
    summed = lax.psum_scatter(
        product.astype(jnp.bfloat16), "head", scatter_dimension=0, tiled=True
    ).astype(jnp.float32)
    layer_out = jnp.transpose(summed, (1, 0, 2)).astype(jnp.bfloat16)
    return (layer_out, state)


def plan(queries, keys, values, token_rates, fast_init, out_gain, out_weight):
    halved = lax.axis_size("ctx") == 2 * BACK and fast_init.shape[1] == 2 and queries.shape[0] == 2
    chosen = shards if halved else shards_any
    return chosen(queries, keys, values, token_rates, fast_init, out_gain, out_weight)


def solution(mesh):
    placed = (
        P(None, "ctx", "head"),
        P(None, "ctx", "head"),
        P(None, "ctx", "head"),
        P(None, "ctx", "head"),
        P(None, "head", None, None),
        P("head"),
        P("head", None),
    )
    return jax.shard_map(
        plan,
        mesh=mesh,
        in_specs=placed,
        out_specs=(P(None, ("ctx", "head"), None), P(None, "head", None, None)),
        check_vma=False,
    )
```

```python
import functools

import jax
import jax.numpy as jnp
from jax import lax
from jax.experimental import pallas as pl
from jax.experimental.pallas import tpu as pltpu
from jax.sharding import PartitionSpec as P

AH = 128
NS_ITERS = 2
BACK = 4


coef_a = 3.4445
coef_b = -4.775
coef_c = 2.0315
LOG2E = 1.4426950408889634
F32 = jnp.float32
BF16 = jnp.bfloat16
NOWHERE = 2**20
VMEM_BYTES = 56 * 1024 * 1024


def swapped(block, mask):
    devices = range(lax.axis_size("ctx"))
    return lax.ppermute(block, "ctx", [(i, i ^ mask) for i in devices])


def raised(block, step):
    devices = range(lax.axis_size("ctx") - step)
    return lax.ppermute(block, "ctx", [(i, i + step) for i in devices])


def after(value, *earlier):
    return lax.optimization_barrier((value,) + earlier)[0]


def rms_inverse(inputs):
    return lax.rsqrt(jnp.mean(inputs * inputs, axis=-1, keepdims=True) + 1e-06)


def sigmoid(inputs):
    return 0.5 * jnp.tanh(0.5 * inputs) + 0.5


def dot_nn(left, right):
    return lax.dot_general(left, right, (((1,), (0,)), ((), ())), preferred_element_type=F32)


def dot_nt(left, right):
    return lax.dot_general(left, right, (((1,), (1,)), ((), ())), preferred_element_type=F32)


def dot_tn(left, right):
    return lax.dot_general(left, right, (((0,), (0,)), ((), ())), preferred_element_type=F32)


def params():
    return pltpu.CompilerParams(vmem_limit_bytes=VMEM_BYTES)


def cost(flops, bytes_accessed, transcendentals=0):
    return pl.CostEstimate(
        flops=flops // 256,
        bytes_accessed=bytes_accessed // 256,
        transcendentals=transcendentals // 256,
    )


def in_vmem(count):
    return [pl.BlockSpec(memory_space=pltpu.VMEM)] * count


IN_SMEM = pl.BlockSpec(memory_space=pltpu.SMEM)


def token_grads(kv_ref, rate_ref, weight_ref, emit):
    keys = kv_ref[0].astype(F32)
    normed = (keys * rms_inverse(keys)).astype(BF16)
    pull = (-rate_ref[:, :1] * kv_ref[1].astype(F32)).astype(BF16)
    first = dot_nn(normed, weight_ref[0])
    third = dot_nn(normed, weight_ref[1])
    back = dot_nt(pull, weight_ref[2])
    sigma = sigmoid(first)
    silu = first * sigma
    hidden = (silu * third).astype(BF16)
    d_third = (back * silu).astype(BF16)
    d_first = (back * third * (sigma * (1.0 + first - silu))).astype(BF16)
    emit(0, dot_tn(normed, d_first))
    emit(1, dot_tn(normed, d_third))
    emit(2, dot_tn(hidden, pull))


def grads_first_kernel(kv_ref, rate_ref, weight_ref, out_ref):
    def emit(index, value):
        out_ref[index] = value

    token_grads(kv_ref, rate_ref, weight_ref, emit)


def grads_second_kernel(core_ref, kv_ref, rate_ref, weight_ref, sum_ref, keep_ref, give_ref, all_ref):
    half = keep_ref.shape[1]
    core = core_ref[0]

    def emit(index, value):
        all_ref[index] = value + sum_ref[index]

    token_grads(kv_ref, rate_ref, weight_ref, emit)
    for index in range(all_ref.shape[0]):
        mine = pl.ds(pl.multiple_of(core * half, half), half)
        other = pl.ds(pl.multiple_of((1 - core) * half, half), half)
        keep_ref[index] = all_ref[index, mine, :].astype(BF16)
        give_ref[index] = all_ref[index, other, :].astype(BF16)


def grads_first(kv, rates, weights):
    tok, width = kv.shape[1:]
    flops = 12 * tok * width * width
    return pl.pallas_call(
        grads_first_kernel,
        out_shape=jax.ShapeDtypeStruct((3, width, width), F32),
        in_specs=in_vmem(3),
        out_specs=in_vmem(1)[0],
        compiler_params=params(),
        cost_estimate=cost(flops, 16 * width * width),
        name="grads_first",
    )(kv, rates, weights)


def grads_second(core, kv, rates, weights, partial):
    tok, width = kv.shape[1:]
    flops = 12 * tok * width * width
    half = jax.ShapeDtypeStruct((3, width // 2, width), BF16)
    return pl.pallas_call(
        grads_second_kernel,
        out_shape=(half, half),
        in_specs=[IN_SMEM] + in_vmem(4),
        out_specs=tuple(in_vmem(2)),
        scratch_shapes=[pltpu.VMEM((3, width, width), F32)],
        compiler_params=params(),
        cost_estimate=cost(flops, 28 * width * width),
        name="grads_second",
    )(core, kv, rates, weights, partial)


def muon_kernel(core_ref, mine_ref, other_ref, *refs, update):
    if update:
        state_ref, ortho_ref, half_ref, weight_ref, grad_ref = refs
    else:
        ortho_ref, half_ref, grad_ref = refs
    half = mine_ref.shape[1]
    core = core_ref[0]
    mine = pl.ds(pl.multiple_of(core * half, half), half)
    other = pl.ds(pl.multiple_of((1 - core) * half, half), half)
    count = mine_ref.shape[0]
    for index in range(count):
        grad_ref[index, mine, :] = mine_ref[index].astype(F32)
        grad_ref[index, other, :] = other_ref[index].astype(F32)
    ortho = []
    for index in range(count):
        grad = grad_ref[index]
        ortho.append((grad * lax.rsqrt(jnp.sum(grad * grad) + 1e-06)).astype(BF16))
    for turn in range(NS_ITERS):
        gram = [dot_tn(mat, mat).astype(BF16) for mat in ortho]
        poly = [(coef_b * mat.astype(F32) + coef_c * dot_nn(mat, mat)).astype(BF16) for mat in gram]
        ortho = [
            (coef_a * mat.astype(F32) + dot_nn(mat, step)).astype(BF16)
            for mat, step in zip(ortho, poly)
        ]
    for index in range(count):
        ortho_ref[index] = ortho[index]
        half_ref[index] = ortho_ref[index, mine, :]
        if update:
            weight_ref[index] = renorm(state_ref[index, 0], ortho[index].astype(F32)).astype(BF16)


def renorm(previous, step):
    fresh = previous - step
    target = jnp.sqrt(jnp.mean(previous * previous, axis=-1, keepdims=True) + 1e-06)
    return fresh * (target * rms_inverse(fresh))


def muon(core, mine, other, state=None, side=None):
    count, half, width = mine.shape
    whole = jax.ShapeDtypeStruct((count, width, width), BF16)
    part = jax.ShapeDtypeStruct((count, half, width), BF16)
    update = state is not None
    outs = (whole, part, whole) if update else (whole, part)
    body = functools.partial(muon_kernel, update=update)
    grid_spec = pltpu.PrefetchScalarGridSpec(
        num_scalar_prefetch=1,
        grid=(1,),
        in_specs=[pl.BlockSpec((count, half, width), lambda i, s: (0, 0, 0))] * 2
        + (
            [pl.BlockSpec((count, 1, width, width), lambda i, s: (0, s[1], 0, 0))]
            if update
            else []
        ),
        out_specs=tuple(pl.BlockSpec(out.shape, lambda i, s: (0, 0, 0)) for out in outs),
        scratch_shapes=[pltpu.VMEM((count, width, width), F32)],
    )
    scalars = jnp.stack([core, core if side is None else side])
    return pl.pallas_call(
        body,
        out_shape=outs,
        grid_spec=grid_spec,
        compiler_params=params(),
        cost_estimate=cost(count * NS_ITERS * 6 * width**3, 12 * width * width),
        name="muon",
    )(scalars, mine, other, *((state,) if update else ()))


def finish_kernel(scalar_ref, state_ref, *refs):
    spans = (len(refs) - 1) // 3
    out_ref = refs[-1]
    core, side = scalar_ref[0], scalar_ref[1]
    half = refs[1].shape[1]
    head = pl.program_id(1)

    def advance(steps):
        value = state_ref[0, 0]
        for step in steps:
            value = renorm(value, step.astype(F32))
        out_ref[0, 0] = value

    @pl.when(head == side)
    def _own():
        advance([refs[3 * span][0] for span in range(spans)])

    @pl.when((head != side) & (core == 0))
    def _first():
        advance(
            [jnp.concatenate([refs[3 * span + 1][0], refs[3 * span + 2][0]], 0) for span in range(spans)]
        )

    @pl.when((head != side) & (core != 0))
    def _second():
        advance(
            [jnp.concatenate([refs[3 * span + 2][0], refs[3 * span + 1][0]], 0) for span in range(spans)]
        )


def finish(core, side, state, steps):
    count, heads, width, _ = state.shape
    half = width // 2
    specs = []
    for _ in steps:
        specs.append(pl.BlockSpec((1, width, width), lambda m, h, s: (m, 0, 0)))
        specs.append(pl.BlockSpec((1, half, width), lambda m, h, s: (m, 0, 0)))
        specs.append(pl.BlockSpec((1, half, width), lambda m, h, s: (m, 0, 0)))
    one = pl.BlockSpec((1, 1, width, width), lambda m, h, s: (m, h, 0, 0))
    grid_spec = pltpu.PrefetchScalarGridSpec(
        num_scalar_prefetch=1,
        grid=(count, heads),
        in_specs=[one] + specs,
        out_specs=one,
    )
    flat = [array for step in steps for array in step]
    return pl.pallas_call(
        finish_kernel,
        out_shape=jax.ShapeDtypeStruct(state.shape, F32),
        grid_spec=grid_spec,
        compiler_params=params(),
        cost_estimate=cost(20 * state.size, 8 * state.size + 4 * state.size),
        name="finish",
    )(jnp.stack([core, side]), state, *flat)


def split_kernel(which_ref, key_away, value_away, key_own, value_own, away_ref, own_ref):
    away_ref[0], away_ref[1] = key_away[0], value_away[0]
    own_ref[0], own_ref[1] = key_own[0], value_own[0]


def split(side, keys, values, span):
    tok, width = keys.shape[1], keys.shape[2] // 2
    rows = tok // 4
    away = pl.BlockSpec((1, rows, width), lambda i, s: (span, i, 1 - s[0]))
    own = pl.BlockSpec((1, rows, width), lambda i, s: (span, i, s[0]))
    out = pl.BlockSpec((2, rows, width), lambda i, s: (0, i, 0))
    shape = jax.ShapeDtypeStruct((2, tok, width), BF16)
    return pl.pallas_call(
        split_kernel,
        out_shape=(shape, shape),
        grid_spec=pltpu.PrefetchScalarGridSpec(
            num_scalar_prefetch=1,
            grid=(tok // rows,),
            in_specs=[away, away, own, own],
            out_specs=(out, out),
        ),
        compiler_params=params(),
        cost_estimate=cost(0, 16 * tok * width),
        name="split",
    )(side[None].astype(jnp.int32), keys, values, keys, values)


def attend_kernel(ids_ref, query_ref, *refs, blocks, pack, at, start, end):
    kv_refs, refs = refs[:blocks], refs[blocks:]
    if not start:
        (sum_in_ref, top_in_ref, fast_ref), refs = refs[:3], refs[3:]
    if end:
        out_ref, refs = refs[0], refs[1:]
    sum_ref, top_ref, bias_ref = refs
    tok = query_ref.shape[1]
    head = pl.program_id(0)
    which = pl.program_id(1)

    @pl.when((head == 0) & (which == 0))
    def _bias():
        row = lax.broadcasted_iota(jnp.int32, (tok, tok), 0)
        column = lax.broadcasted_iota(jnp.int32, (tok, tok), 1)
        bias_ref[0] = jnp.where(column <= row, 0.0, -1e30)
        bias_ref[1] = jnp.zeros((tok, tok), F32)
        bias_ref[2] = jnp.where(column > row, 0.0, -1e30)

    if start:
        sum_ref[...] = jnp.zeros_like(sum_ref)
        top_ref[...] = jnp.full_like(top_ref, -1e30)
    else:
        sum_ref[...] = sum_in_ref[...]
        top_ref[...] = top_in_ref[...]
    place = ids_ref[which + at]
    ones = jnp.ones((tok, AH), BF16)
    scale = AH**-0.5 * LOG2E
    for block in range(blocks):
        apart = place - ids_ref[2 + block]

        @pl.when((apart >= 0) & (apart <= BACK))
        def _block(block=block, apart=apart):
            kind = jnp.where(apart == 0, 0, jnp.where(apart == BACK, 2, 1))
            scores = []
            for one in range(pack):
                lanes = slice(one * AH, (one + 1) * AH)
                product = dot_nt(query_ref[0, :, lanes], kv_refs[block][0, :, lanes])
                scores.append(product + bias_ref[kind])
            for one in range(pack):
                lanes = slice(one * AH, (one + 1) * AH)
                old = top_ref[one, 0]
                top = jnp.maximum(old, jnp.max(scores[one], axis=-1, keepdims=True))
                weights = [
                    jnp.exp2((scores[one][:, low : low + AH] - top) * scale)
                    for low in range(0, tok, AH)
                ]
                weights = jnp.concatenate(weights, 1).astype(BF16)
                shrink = jnp.exp2((old - top) * scale)
                fresh = dot_nn(weights, jnp.concatenate([kv_refs[block][1, :, lanes], ones], 1))
                sum_ref[one, 0, :, :AH] = sum_ref[one, 0, :, :AH] * shrink + fresh[:, :AH]
                sum_ref[one, 0, :, AH:] = sum_ref[one, 0, :, AH:] * shrink + fresh[:, AH:]
                top_ref[one, 0] = top

    if end:
        for one in range(pack):
            lanes = slice(one * AH, (one + 1) * AH)
            attn = sum_ref[one, 0, :, :AH] / sum_ref[one, 0, :, AH:]
            out_ref[0, :, lanes] = (fast_ref[0, :, lanes] + attn).astype(BF16)


def attend(ids, queries, kvs, carry=None, fast=None, only=None):
    two, tok, features = queries.shape
    at = 0 if only is None else only
    count = two if only is None else 1
    end = carry is not None
    heads = features // AH
    pack = 2
    blocks = len(kvs)
    start = carry is None
    query_spec = pl.BlockSpec((1, tok, pack * AH), lambda h, w, s: (w + at, 0, h))
    kv_spec = pl.BlockSpec((2, tok, pack * AH), lambda h, w, s: (0, 0, h))
    sum_block, top_block = (pack, 1, tok, 2 * AH), (pack, 1, tok, AH)
    sum_spec = pl.BlockSpec(sum_block, lambda h, w, s: (h, w + at, 0, 0))
    top_spec = pl.BlockSpec(top_block, lambda h, w, s: (h, w + at, 0, 0))
    sum_shape = jax.ShapeDtypeStruct((heads, two, tok, 2 * AH), F32)
    top_shape = jax.ShapeDtypeStruct((heads, two, tok, AH), F32)
    scratch = [pltpu.VMEM((3, tok, tok), F32)]
    if end:
        outs = jax.ShapeDtypeStruct((count, tok, features), BF16)
        out_specs = pl.BlockSpec((1, tok, pack * AH), lambda h, w, s: (w, 0, h))
        scratch = [pltpu.VMEM(sum_block, F32), pltpu.VMEM(top_block, F32)] + scratch
    else:
        outs, out_specs = (sum_shape, top_shape), (sum_spec, top_spec)
    grid_spec = pltpu.PrefetchScalarGridSpec(
        num_scalar_prefetch=1,
        grid=(heads // pack, count),
        in_specs=[query_spec] + [kv_spec] * blocks + ([] if start else [sum_spec, top_spec, query_spec]),
        out_specs=out_specs,
        scratch_shapes=scratch,
    )
    pairs = heads * 5 * count // 2
    return pl.pallas_call(
        functools.partial(attend_kernel, blocks=blocks, pack=pack, at=at, start=start, end=end),
        out_shape=outs,
        grid_spec=grid_spec,
        compiler_params=params(),
        cost_estimate=cost(
            pairs * 8 * tok * tok * AH, blocks * 4 * tok * features, pairs * tok * tok
        ),
        name="attend",
    )(ids, queries, *kvs, *(() if start else (*carry, fast)))


def answer_kernel(query_ref, weight_ref, gain_ref, out_ref):
    query = query_ref[0].astype(F32)
    normed = (query * rms_inverse(query)).astype(BF16)
    first = dot_nn(normed, weight_ref[0])
    third = dot_nn(normed, weight_ref[1])
    hidden = (first * sigmoid(first) * third).astype(BF16)
    answer = dot_nn(hidden, weight_ref[2])
    out_ref[0] = answer * rms_inverse(answer) * gain_ref[...]


def answer(queries, weights, gain):
    two, tok, width = queries.shape
    block = pl.BlockSpec((1, tok, width), lambda w: (w, 0, 0))
    return pl.pallas_call(
        answer_kernel,
        out_shape=jax.ShapeDtypeStruct(queries.shape, F32),
        grid=(two,),
        in_specs=[
            block,
            pl.BlockSpec(weights.shape, lambda w: (0, 0, 0)),
            pl.BlockSpec((1, width), lambda w: (0, 0)),
        ],
        out_specs=block,
        compiler_params=params(),
        cost_estimate=cost(two * 6 * tok * width * width, 10 * tok * width),
        name="answer",
    )(queries, weights, gain)


def project_kernel(which_ref, own_ref, got_ref, own_weight_ref, got_weight_ref, out_ref):
    total = dot_nn(own_ref[0], own_weight_ref[...]) + dot_nn(got_ref[0], got_weight_ref[...])
    out_ref[...] = total.astype(BF16)


def project(which, own, got, weight):
    count, depth = own.shape[1:]
    columns = weight.shape[1]
    wide = 512
    rows = pl.BlockSpec((1, count, depth), lambda i, s: (0, 0, 0))
    grid_spec = pltpu.PrefetchScalarGridSpec(
        num_scalar_prefetch=1,
        grid=(columns // wide,),
        in_specs=[
            rows,
            rows,
            pl.BlockSpec((depth, wide), lambda i, s: (s[0], i)),
            pl.BlockSpec((depth, wide), lambda i, s: (1 - s[0], i)),
        ],
        out_specs=pl.BlockSpec((count, wide), lambda i, s: (0, i)),
    )
    return pl.pallas_call(
        project_kernel,
        out_shape=jax.ShapeDtypeStruct((count, columns), BF16),
        grid_spec=grid_spec,
        compiler_params=params(),
        cost_estimate=cost(4 * count * depth * columns, 4 * depth * columns),
        name="project",
    )(which[None].astype(jnp.int32), own, got, weight, weight)


def shards(queries, keys, values, token_rates, fast_init, out_gain, out_weight):
    spans, tok, features = queries.shape
    width = fast_init.shape[2]
    position = lax.axis_index("ctx")
    around = lax.axis_size("ctx")
    upper = around // 2
    core = position % 2
    side = (position // 2) % 2
    far = position // upper
    here = side == 0
    core_one = core[None].astype(jnp.int32)

    def keep(array):
        return jnp.where(here, array[..., :width], array[..., width:])

    def give(array):
        return jnp.where(here, array[..., width:], array[..., :width])

    def column(rates):
        return jnp.broadcast_to(rates[:, None], (tok, 128))

    def added(left, right):
        return (left.astype(F32) + right.astype(F32)).astype(BF16)

    own_place = 2 * side + core
    got_place = 2 * (1 - side) + core
    own_pair = 2 * side + 1 - core
    got_pair = 2 * (1 - side) + 1 - core
    places = jnp.stack([own_place, got_place, own_pair, got_pair]).astype(jnp.int32)

    def ids(span, *bases):
        mine = span * around + far * upper + places[:2]
        return jnp.concatenate([mine] + [base + places for base in bases]).astype(jnp.int32)

    def total_over_heads(product):
        return lax.psum_scatter(product, "head", scatter_dimension=0, tiled=True)

    kv_away0, kv_own0 = split(side, keys, values, 0)
    kv_got0 = swapped(kv_away0, 2)
    far_own0 = swapped(kv_own0, upper)
    pair_own0 = swapped(kv_own0, 1)
    rates_away = jnp.where(here, token_rates[..., 1], token_rates[..., 0])
    rates_got = swapped(rates_away, 2)
    rates_own = jnp.where(here, token_rates[..., 0], token_rates[..., 1])
    weights0 = jnp.where(here, fast_init[:, 0], fast_init[:, 1]).astype(BF16)
    gain = keep(out_gain[None, :])
    partial0 = grads_first(kv_own0, column(rates_own[0]), weights0)

    query_got0 = swapped(after(give(queries[0]), kv_got0, partial0), 2)
    far_got0 = swapped(after(kv_got0, far_own0, partial0), upper)
    pair_got0 = swapped(after(kv_got0, partial0), 1)
    kv_away1, kv_own1 = split(after(side, partial0), keys, values, 1)
    kv_got1 = swapped(after(kv_away1, query_got0), 2)
    keep0, give0 = grads_second(
        after(core_one, partial0, kv_own1, query_got0), kv_got0, column(rates_got[0]), weights0, partial0
    )
    chip0 = added(keep0, swapped(give0, 1))
    query0 = jnp.stack([keep(queries[0]), query_got0])
    near0 = attend(
        after(ids(0, far * upper), keep0), query0, [kv_own0, kv_got0, pair_own0, pair_got0]
    )
    pair_far_own0 = swapped(far_own0, 1)
    pair_far_got0 = swapped(after(far_got0, near0[1]), 1)
    fast0 = answer(after(query0, near0[1], chip0), weights0, gain)
    other0 = swapped(after(chip0, far_got0, near0[1]), upper)
    fars0 = [far_own0, far_got0, pair_far_own0, pair_far_got0]
    late = jnp.where(far == 0, NOWHERE, 0)
    ids0 = ids(0, late)
    mixed_got0 = attend(after(ids0, fast0, kv_got1), query0, fars0, near0, fast0, 1)
    returned0 = swapped(mixed_got0, 2)
    far_own1 = raised(after(kv_own1, other0, mixed_got0), upper)
    total0 = added(chip0, after(other0, mixed_got0))
    pair_total0 = swapped(total0, 1)
    mixed_own0 = attend(after(ids0, mixed_got0, total0), query0, fars0, near0, fast0, 0)
    product0 = project(side, mixed_own0, returned0, out_weight)
    layer0 = total_over_heads(after(product0, far_own1))

    query_got1 = swapped(after(give(queries[1]), kv_got1, returned0), 2)
    ortho0, half0, weights1 = muon(after(core, product0), total0, pair_total0, fast_init, side)
    pair_own1 = swapped(after(kv_own1, product0), 1)
    pair_got1 = swapped(after(kv_got1, product0), 1)
    partial1 = grads_first(
        kv_own1, column(rates_own[1]), after(weights1, query_got1)
    )
    far_got1 = raised(after(kv_got1, far_own1, product0), upper)
    keep1, give1 = grads_second(
        after(core_one, partial1), kv_got1, column(rates_got[1]), weights1, partial1
    )
    chip1 = added(keep1, swapped(give1, 1))
    away0 = swapped(after(half0, query_got1, keep1), 2)
    pair_far_own1 = swapped(after(far_own1, keep1), 1)
    query1 = jnp.stack([keep(queries[1]), query_got1])
    fast1 = answer(after(query1, keep1), weights1, gain)
    near1 = attend(
        after(ids(1, around + far * upper), fast1),
        query1,
        [kv_own1, kv_got1, pair_own1, pair_got1],
    )
    pair_far_got1 = swapped(after(far_got1, fast1), 1)
    other1 = swapped(after(chip1, far_got1, near1[1]), upper)
    fars1 = [far_own1, far_got1, pair_far_own1, pair_far_got1]
    early = jnp.where(far == 0, around - upper, NOWHERE)
    late = jnp.where(far == 0, NOWHERE, around)
    ids1 = ids(1, early, late)
    mixed_got1 = attend(after(ids1, near1[1]), query1, fars0 + fars1, near1, fast1, 1)
    returned1 = swapped(mixed_got1, 2)
    mixed_own1 = attend(after(ids1, mixed_got1, other1), query1, fars0 + fars1, near1, fast1, 0)
    product1 = project(side, mixed_own1, returned1, out_weight)
    total1 = added(chip1, after(other1, product1))
    pair_total1 = swapped(total1, 1)
    pair_away0 = swapped(after(away0, product1), 1)
    layer1 = total_over_heads(product1)

    ortho1, half1 = muon(after(core, product1), total1, pair_total1)
    away1 = swapped(half1, 2)
    steps = [(ortho0, away0, pair_away0), (ortho1, away1, swapped(away1, 1))]
    state = finish(core, side, fast_init, steps)
    return (jnp.stack([layer0, layer1], 0), state)


def shifted(block, axis, distance):
    devices = range(lax.axis_size(axis))
    route = [((i - distance) % len(devices), i) for i in devices]
    return lax.ppermute(block, axis, route)


def head_norm(inputs):
    return inputs / jnp.sqrt(jnp.mean(inputs * inputs, axis=-1, keepdims=True) + 1e-06)


def renormed(previous, fresh):
    target = jnp.sqrt(jnp.mean(previous * previous, axis=-1, keepdims=True) + 1e-06)
    actual = jnp.sqrt(jnp.mean(fresh * fresh, axis=-1, keepdims=True) + 1e-06)
    return fresh * target / actual


def newton_turn(ortho, gram):
    gram_bf = gram.astype(jnp.bfloat16)
    square = jnp.einsum("mhij,mhjk->mhik", gram_bf, gram_bf, preferred_element_type=jnp.float32)
    poly = (coef_b * gram_bf.astype(jnp.float32) + coef_c * square).astype(jnp.bfloat16)
    moved = jnp.einsum("rmhi,mhij->rmhj", ortho, poly, preferred_element_type=jnp.float32)
    return (coef_a * ortho.astype(jnp.float32) + moved).astype(jnp.bfloat16)


def fix_wrapped(received, distance, position):
    rolled = jnp.concatenate([jnp.zeros_like(received[:1]), received[:-1]], 0)
    return jnp.where(position < distance, rolled, received)


def shards_any(queries, keys, values, token_rates, fast_init, out_gain, out_weight):
    spans, tok, features = queries.shape
    per_dev = fast_init.shape[1]
    width = fast_init.shape[2]
    att_heads = features // AH
    position = lax.axis_index("ctx")
    far_keys = []
    far_values = []
    carried = (keys, values)
    for distance in (1, 2, 3, 4):
        carried = shifted((carried[0], carried[1]), "ctx", 1)
        far_keys.insert(0, fix_wrapped(carried[0], distance, position))
        far_values.insert(0, fix_wrapped(carried[1], distance, position))
    window_keys = jnp.concatenate(far_keys + [keys], 1)
    window_values = jnp.concatenate(far_values + [values], 1)
    scale = AH ** (-0.5)
    query_pos = jnp.arange(tok, dtype=jnp.int32)[:, None]
    key_pos = jnp.arange(5 * tok, dtype=jnp.int32)[None, :]
    distance_pos = query_pos + 4 * tok - key_pos
    in_window = (distance_pos >= 0) & (distance_pos < 4 * tok)
    key_shard = 4 - key_pos // tok
    gain = out_gain.reshape(per_dev, width)
    state = fast_init
    mixed_all = []
    for span in range(spans):
        valid = in_window
        if span == 0:
            valid = valid & jnp.logical_not(position < key_shard)
        query_heads = queries[span].reshape(tok, att_heads, AH)
        key_heads = window_keys[span].reshape(5 * tok, att_heads, AH)
        value_heads = window_values[span].reshape(5 * tok, att_heads, AH)
        scores = (
            jnp.einsum("qnd,knd->nqk", query_heads, key_heads, preferred_element_type=jnp.float32)
            * scale
        )
        scores = jnp.where(valid[None], scores, -1e30)
        largest = jnp.max(scores, axis=-1, keepdims=True)
        expon = jnp.exp(scores - largest)
        probs = (expon / jnp.sum(expon, axis=-1, keepdims=True)).astype(jnp.bfloat16)
        attn = jnp.einsum(
            "nqk,knd->qnd", probs, value_heads, preferred_element_type=jnp.float32
        ).reshape(tok, features)
        query_norm = head_norm(
            queries[span].reshape(tok, per_dev, width).astype(jnp.float32)
        ).astype(jnp.bfloat16)
        key_norm = head_norm(keys[span].reshape(tok, per_dev, width).astype(jnp.float32)).astype(
            jnp.bfloat16
        )
        value_own = values[span].reshape(tok, per_dev, width)
        weights_bf = state.astype(jnp.bfloat16)
        q_first = jnp.einsum(
            "shd,hde->she", query_norm, weights_bf[0], preferred_element_type=jnp.float32
        )
        q_third = jnp.einsum(
            "shd,hde->she", query_norm, weights_bf[1], preferred_element_type=jnp.float32
        )
        query_hidden = (q_first * jax.nn.sigmoid(q_first) * q_third).astype(jnp.bfloat16)
        fast_out = jnp.einsum(
            "she,hed->shd", query_hidden, weights_bf[2], preferred_element_type=jnp.float32
        )
        first = jnp.einsum(
            "shd,hde->she", key_norm, weights_bf[0], preferred_element_type=jnp.float32
        )
        third = jnp.einsum(
            "shd,hde->she", key_norm, weights_bf[1], preferred_element_type=jnp.float32
        )
        sigma = jax.nn.sigmoid(first)
        key_hidden = (first * sigma * third).astype(jnp.bfloat16)
        pull = (-token_rates[span][:, :, None] * value_own.astype(jnp.float32)).astype(jnp.bfloat16)
        back = jnp.einsum("shd,hed->she", pull, weights_bf[2], preferred_element_type=jnp.float32)
        d_first = (back * third * sigma * (1.0 + first * (1.0 - sigma))).astype(jnp.bfloat16)
        d_third = (back * first * sigma).astype(jnp.bfloat16)
        grad_first = jnp.einsum(
            "shr,she->rhe", key_norm, d_first, preferred_element_type=jnp.float32
        )
        grad_third = jnp.einsum(
            "shr,she->rhe", key_norm, d_third, preferred_element_type=jnp.float32
        )
        grad_down = jnp.einsum("shr,shd->rhd", key_hidden, pull, preferred_element_type=jnp.float32)
        grad_rows = lax.psum_scatter(
            jnp.stack([grad_first, grad_third, grad_down], 1).astype(jnp.bfloat16),
            "ctx",
            scatter_dimension=0,
            tiled=True,
        ).astype(jnp.float32)
        squares = lax.psum(jnp.sum(grad_rows * grad_rows, axis=(0, 3)), "ctx")
        ortho_rows = (grad_rows * lax.rsqrt(squares + 1e-06)[None, :, :, None]).astype(jnp.bfloat16)
        ortho = lax.all_gather(ortho_rows, "ctx", axis=0, tiled=True)
        for turn in range(NS_ITERS):
            gram = jnp.einsum("rmhi,rmhj->mhij", ortho, ortho, preferred_element_type=jnp.float32)
            ortho = newton_turn(ortho, gram)
        ortho_mats = jnp.transpose(ortho, (1, 2, 0, 3)).astype(jnp.float32)
        state = renormed(state, state - ortho_mats)
        normed = head_norm(fast_out) * gain
        mixed_all.append((normed.reshape(tok, features) + attn).astype(jnp.bfloat16))
    combined = jnp.stack(mixed_all, 0)
    product = jnp.einsum("ctd,de->tce", combined, out_weight, preferred_element_type=jnp.float32)
    summed = lax.psum_scatter(
        product.astype(jnp.bfloat16), "head", scatter_dimension=0, tiled=True
    ).astype(jnp.float32)
    layer_out = jnp.transpose(summed, (1, 0, 2)).astype(jnp.bfloat16)
    return (layer_out, state)


def plan(queries, keys, values, token_rates, fast_init, out_gain, out_weight):
    halved = lax.axis_size("ctx") == 2 * BACK and fast_init.shape[1] == 2 and queries.shape[0] == 2
    chosen = shards if halved else shards_any
    return chosen(queries, keys, values, token_rates, fast_init, out_gain, out_weight)


def solution(mesh):
    placed = (
        P(None, "ctx", "head"),
        P(None, "ctx", "head"),
        P(None, "ctx", "head"),
        P(None, "ctx", "head"),
        P(None, "head", None, None),
        P("head"),
        P("head", None),
    )
    return jax.shard_map(
        plan,
        mesh=mesh,
        in_specs=placed,
        out_specs=(P(None, ("ctx", "head"), None), P(None, "head", None, None)),
        check_vma=False,
    )
```

```python
import functools

import jax
import jax.numpy as jnp
from jax import lax
from jax.experimental import pallas as pl
from jax.experimental.pallas import tpu as pltpu
from jax.sharding import PartitionSpec as P

AH = 128
NS_ITERS = 2
BACK = 4


coef_a = 3.4445
coef_b = -4.775
coef_c = 2.0315
LOG2E = 1.4426950408889634
F32 = jnp.float32
BF16 = jnp.bfloat16
NOWHERE = 2**20
VMEM_BYTES = 62 * 1024 * 1024


def swapped(block, mask):
    devices = range(lax.axis_size("ctx"))
    return lax.ppermute(block, "ctx", [(i, i ^ mask) for i in devices])


def raised(block, step):
    devices = range(lax.axis_size("ctx") - step)
    return lax.ppermute(block, "ctx", [(i, i + step) for i in devices])


def after(value, *earlier):
    return lax.optimization_barrier((value,) + earlier)[0]


def rms_inverse(inputs):
    return lax.rsqrt(jnp.mean(inputs * inputs, axis=-1, keepdims=True) + 1e-06)


def sigmoid(inputs):
    return 0.5 * jnp.tanh(0.5 * inputs) + 0.5


def dot_nn(left, right):
    return lax.dot_general(left, right, (((1,), (0,)), ((), ())), preferred_element_type=F32)


def dot_nt(left, right):
    return lax.dot_general(left, right, (((1,), (1,)), ((), ())), preferred_element_type=F32)


def dot_tn(left, right):
    return lax.dot_general(left, right, (((0,), (0,)), ((), ())), preferred_element_type=F32)


def params():
    return pltpu.CompilerParams(vmem_limit_bytes=VMEM_BYTES)


def cost(flops, bytes_accessed, transcendentals=0):
    return pl.CostEstimate(
        flops=flops // 256,
        bytes_accessed=bytes_accessed // 256,
        transcendentals=transcendentals // 256,
    )


def in_vmem(count):
    return [pl.BlockSpec(memory_space=pltpu.VMEM)] * count


IN_SMEM = pl.BlockSpec(memory_space=pltpu.SMEM)


def token_grads(kv_ref, rate_ref, weight_ref, emit):
    keys = kv_ref[0].astype(F32)
    normed = (keys * rms_inverse(keys)).astype(BF16)
    pull = (-rate_ref[:, :1] * kv_ref[1].astype(F32)).astype(BF16)
    first = dot_nn(normed, weight_ref[0])
    third = dot_nn(normed, weight_ref[1])
    back = dot_nt(pull, weight_ref[2])
    sigma = sigmoid(first)
    silu = first * sigma
    hidden = (silu * third).astype(BF16)
    d_third = (back * silu).astype(BF16)
    d_first = (back * third * (sigma * (1.0 + first - silu))).astype(BF16)
    emit(0, dot_tn(normed, d_first))
    emit(1, dot_tn(normed, d_third))
    emit(2, dot_tn(hidden, pull))


def grads_first_kernel(kv_ref, rate_ref, weight_ref, out_ref):
    def emit(index, value):
        out_ref[index] = value

    token_grads(kv_ref, rate_ref, weight_ref, emit)


def grads_second_kernel(core_ref, kv_ref, rate_ref, weight_ref, sum_ref, keep_ref, give_ref, all_ref):
    def emit(index, value):
        all_ref[index] = value + sum_ref[index]

    token_grads(kv_ref, rate_ref, weight_ref, emit)
    halve(core_ref[0], all_ref, keep_ref, give_ref)


def grads_both_kernel(core_ref, own_ref, own_rate, got_ref, got_rate, weight_ref, *refs):
    keep_ref, give_ref, all_ref = refs

    def emit(index, value):
        all_ref[index] = value

    def add(index, value):
        all_ref[index] += value

    token_grads(own_ref, own_rate, weight_ref, emit)
    token_grads(got_ref, got_rate, weight_ref, add)
    halve(core_ref[0], all_ref, keep_ref, give_ref)


def halve(core, all_ref, keep_ref, give_ref):
    half = keep_ref.shape[1]
    for index in range(all_ref.shape[0]):
        mine = pl.ds(pl.multiple_of(core * half, half), half)
        other = pl.ds(pl.multiple_of((1 - core) * half, half), half)
        keep_ref[index] = all_ref[index, mine, :].astype(BF16)
        give_ref[index] = all_ref[index, other, :].astype(BF16)


def grads_first(kv, rates, weights):
    tok, width = kv.shape[1:]
    flops = 12 * tok * width * width
    return pl.pallas_call(
        grads_first_kernel,
        out_shape=jax.ShapeDtypeStruct((3, width, width), F32),
        in_specs=in_vmem(3),
        out_specs=in_vmem(1)[0],
        compiler_params=params(),
        cost_estimate=cost(flops, 16 * width * width),
        name="grads_first",
    )(kv, rates, weights)


def grads_second(core, kv, rates, weights, partial):
    tok, width = kv.shape[1:]
    flops = 12 * tok * width * width
    half = jax.ShapeDtypeStruct((3, width // 2, width), BF16)
    return pl.pallas_call(
        grads_second_kernel,
        out_shape=(half, half),
        in_specs=[IN_SMEM] + in_vmem(4),
        out_specs=tuple(in_vmem(2)),
        scratch_shapes=[pltpu.VMEM((3, width, width), F32)],
        compiler_params=params(),
        cost_estimate=cost(flops, 28 * width * width),
        name="grads_second",
    )(core, kv, rates, weights, partial)


def grads_both(core, kv_own, rates_own, kv_got, rates_got, weights):
    tok, width = kv_own.shape[1:]
    half = jax.ShapeDtypeStruct((3, width // 2, width), BF16)
    return pl.pallas_call(
        grads_both_kernel,
        out_shape=(half, half),
        in_specs=[IN_SMEM] + in_vmem(5),
        out_specs=tuple(in_vmem(2)),
        scratch_shapes=[pltpu.VMEM((3, width, width), F32)],
        compiler_params=params(),
        cost_estimate=cost(24 * tok * width * width, 20 * width * width),
        name="grads_both",
    )(core, kv_own, rates_own, kv_got, rates_got, weights)


def muon_kernel(core_ref, mine_ref, other_ref, *refs, update):
    if update:
        state_ref, ortho_ref, half_ref, weight_ref, grad_ref = refs
    else:
        ortho_ref, half_ref, grad_ref = refs
    half = mine_ref.shape[1]
    core = core_ref[0]
    mine = pl.ds(pl.multiple_of(core * half, half), half)
    other = pl.ds(pl.multiple_of((1 - core) * half, half), half)
    count = mine_ref.shape[0]
    for index in range(count):
        grad_ref[index, mine, :] = mine_ref[index].astype(F32)
        grad_ref[index, other, :] = other_ref[index].astype(F32)
    ortho = []
    for index in range(count):
        grad = grad_ref[index]
        ortho.append((grad * lax.rsqrt(jnp.sum(grad * grad) + 1e-06)).astype(BF16))
    for turn in range(NS_ITERS):
        gram = [dot_tn(mat, mat).astype(BF16) for mat in ortho]
        poly = [(coef_b * mat.astype(F32) + coef_c * dot_nn(mat, mat)).astype(BF16) for mat in gram]
        ortho = [
            (coef_a * mat.astype(F32) + dot_nn(mat, step)).astype(BF16)
            for mat, step in zip(ortho, poly)
        ]
    for index in range(count):
        ortho_ref[index] = ortho[index]
        half_ref[index] = ortho_ref[index, mine, :]
        if update:
            weight_ref[index] = renorm(state_ref[index, 0], ortho[index].astype(F32)).astype(BF16)


def renorm(previous, step):
    fresh = previous - step
    target = jnp.sqrt(jnp.mean(previous * previous, axis=-1, keepdims=True) + 1e-06)
    return fresh * (target * rms_inverse(fresh))


def muon(core, mine, other, state=None, side=None):
    count, half, width = mine.shape
    whole = jax.ShapeDtypeStruct((count, width, width), BF16)
    part = jax.ShapeDtypeStruct((count, half, width), BF16)
    update = state is not None
    outs = (whole, part, whole) if update else (whole, part)
    body = functools.partial(muon_kernel, update=update)
    grid_spec = pltpu.PrefetchScalarGridSpec(
        num_scalar_prefetch=1,
        grid=(1,),
        in_specs=[pl.BlockSpec((count, half, width), lambda i, s: (0, 0, 0))] * 2
        + (
            [pl.BlockSpec((count, 1, width, width), lambda i, s: (0, s[1], 0, 0))]
            if update
            else []
        ),
        out_specs=tuple(pl.BlockSpec(out.shape, lambda i, s: (0, 0, 0)) for out in outs),
        scratch_shapes=[pltpu.VMEM((count, width, width), F32)],
    )
    scalars = jnp.stack([core, core if side is None else side])
    return pl.pallas_call(
        body,
        out_shape=outs,
        grid_spec=grid_spec,
        compiler_params=params(),
        cost_estimate=cost(count * NS_ITERS * 6 * width**3, 12 * width * width),
        name="muon",
    )(scalars, mine, other, *((state,) if update else ()))


def advance(state_ref, out_ref, steps):
    value = state_ref[0, 0]
    for step in steps:
        value = renorm(value, step.astype(F32))
    out_ref[0, 0] = value


def finish_own_kernel(scalar_ref, state_ref, *refs):
    advance(state_ref, refs[-1], [ref[0] for ref in refs[:-1]])


def finish_other_kernel(scalar_ref, state_ref, done_ref, *refs):
    core = scalar_ref[0]
    out_ref = refs[-1]
    pairs = [(refs[at][0], refs[at + 1][0]) for at in range(0, len(refs) - 1, 2)]

    @pl.when(core == 0)
    def _first():
        advance(state_ref, out_ref, [jnp.concatenate([low, high], 0) for low, high in pairs])

    @pl.when(core != 0)
    def _second():
        advance(state_ref, out_ref, [jnp.concatenate([high, low], 0) for low, high in pairs])


def finish(core, side, state, steps, done=None):
    count, _, width, _ = state.shape
    other = done is not None
    rows = width // 2 if other else width
    block = (1, 1, width, width)
    if other:
        one = pl.BlockSpec(block, lambda m, s: (m, 1 - s[1], 0, 0))
    else:
        one = pl.BlockSpec(block, lambda m, s: (m, s[1], 0, 0))
    grid_spec = pltpu.PrefetchScalarGridSpec(
        num_scalar_prefetch=1,
        grid=(count,),
        in_specs=[one]
        + [pl.BlockSpec(memory_space=pl.ANY)] * other
        + [pl.BlockSpec((1, rows, width), lambda m, s: (m, 0, 0))] * len(steps),
        out_specs=one,
    )
    return pl.pallas_call(
        finish_other_kernel if other else finish_own_kernel,
        out_shape=jax.ShapeDtypeStruct(state.shape, F32),
        grid_spec=grid_spec,
        input_output_aliases={2: 0} if other else {},
        compiler_params=params(),
        cost_estimate=cost(10 * state.size, 6 * state.size),
        name="finish",
    )(jnp.stack([core, side]), state, *((done,) if other else ()), *steps)


def split_kernel(which_ref, key_away, value_away, key_own, value_own, away_ref, own_ref):
    away_ref[0], away_ref[1] = key_away[0], value_away[0]
    own_ref[0], own_ref[1] = key_own[0], value_own[0]


def split(side, keys, values, span):
    tok, width = keys.shape[1], keys.shape[2] // 2
    rows = tok // 4
    away = pl.BlockSpec((1, rows, width), lambda i, s: (span, i, 1 - s[0]))
    own = pl.BlockSpec((1, rows, width), lambda i, s: (span, i, s[0]))
    out = pl.BlockSpec((2, rows, width), lambda i, s: (0, i, 0))
    shape = jax.ShapeDtypeStruct((2, tok, width), BF16)
    return pl.pallas_call(
        split_kernel,
        out_shape=(shape, shape),
        grid_spec=pltpu.PrefetchScalarGridSpec(
            num_scalar_prefetch=1,
            grid=(tok // rows,),
            in_specs=[away, away, own, own],
            out_specs=(out, out),
        ),
        compiler_params=params(),
        cost_estimate=cost(0, 16 * tok * width),
        name="split",
    )(side[None].astype(jnp.int32), keys, values, keys, values)


def attend_kernel(ids_ref, query_ref, *refs, blocks, pack, at, start, end):
    kv_refs, refs = refs[:blocks], refs[blocks:]
    if not start:
        (sum_in_ref, top_in_ref, fast_ref), refs = refs[:3], refs[3:]
    if end:
        out_ref, refs = refs[0], refs[1:]
    sum_ref, top_ref, bias_ref = refs
    tok = query_ref.shape[1]
    head = pl.program_id(0)
    which = pl.program_id(1)

    @pl.when((head == 0) & (which == 0))
    def _bias():
        row = lax.broadcasted_iota(jnp.int32, (tok, tok), 0)
        column = lax.broadcasted_iota(jnp.int32, (tok, tok), 1)
        bias_ref[0] = jnp.where(column <= row, 0.0, -1e30)
        bias_ref[1] = jnp.zeros((tok, tok), F32)
        bias_ref[2] = jnp.where(column > row, 0.0, -1e30)

    if start:
        sum_ref[...] = jnp.zeros_like(sum_ref)
        top_ref[...] = jnp.full_like(top_ref, -1e30)
    else:
        sum_ref[...] = sum_in_ref[...]
        top_ref[...] = top_in_ref[...]
    place = ids_ref[which + at]
    ones = jnp.ones((tok, AH), BF16)
    scale = AH**-0.5 * LOG2E
    for block in range(blocks):
        apart = place - ids_ref[2 + block]

        @pl.when((apart >= 0) & (apart <= BACK))
        def _block(block=block, apart=apart):
            kind = jnp.where(apart == 0, 0, jnp.where(apart == BACK, 2, 1))
            scores = []
            for one in range(pack):
                lanes = slice(one * AH, (one + 1) * AH)
                product = dot_nt(query_ref[0, :, lanes], kv_refs[block][0, :, lanes])
                scores.append(product + bias_ref[kind])
            for one in range(pack):
                lanes = slice(one * AH, (one + 1) * AH)
                old = top_ref[one, 0]
                top = jnp.maximum(old, jnp.max(scores[one], axis=-1, keepdims=True))
                weights = [
                    jnp.exp2((scores[one][:, low : low + AH] - top) * scale)
                    for low in range(0, tok, AH)
                ]
                weights = jnp.concatenate(weights, 1).astype(BF16)
                shrink = jnp.exp2((old - top) * scale)
                fresh = dot_nn(weights, jnp.concatenate([kv_refs[block][1, :, lanes], ones], 1))
                sum_ref[one, 0, :, :AH] = sum_ref[one, 0, :, :AH] * shrink + fresh[:, :AH]
                sum_ref[one, 0, :, AH:] = sum_ref[one, 0, :, AH:] * shrink + fresh[:, AH:]
                top_ref[one, 0] = top

    if end:
        for one in range(pack):
            lanes = slice(one * AH, (one + 1) * AH)
            attn = sum_ref[one, 0, :, :AH] / sum_ref[one, 0, :, AH:]
            out_ref[0, :, lanes] = (fast_ref[0, :, lanes] + attn).astype(BF16)


def attend(ids, queries, kvs, carry=None, fast=None, only=None):
    two, tok, features = queries.shape
    at = 0 if only is None else only
    count = two if only is None else 1
    end = carry is not None
    heads = features // AH
    pack = 2
    blocks = len(kvs)
    start = carry is None
    query_spec = pl.BlockSpec((1, tok, pack * AH), lambda h, w, s: (w + at, 0, h))
    kv_spec = pl.BlockSpec((2, tok, pack * AH), lambda h, w, s: (0, 0, h))
    sum_block, top_block = (pack, 1, tok, 2 * AH), (pack, 1, tok, AH)
    sum_spec = pl.BlockSpec(sum_block, lambda h, w, s: (h, w + at, 0, 0))
    top_spec = pl.BlockSpec(top_block, lambda h, w, s: (h, w + at, 0, 0))
    sum_shape = jax.ShapeDtypeStruct((heads, two, tok, 2 * AH), F32)
    top_shape = jax.ShapeDtypeStruct((heads, two, tok, AH), F32)
    scratch = [pltpu.VMEM((3, tok, tok), F32)]
    if end:
        outs = jax.ShapeDtypeStruct((count, tok, features), BF16)
        out_specs = pl.BlockSpec((1, tok, pack * AH), lambda h, w, s: (w, 0, h))
        scratch = [pltpu.VMEM(sum_block, F32), pltpu.VMEM(top_block, F32)] + scratch
    else:
        outs, out_specs = (sum_shape, top_shape), (sum_spec, top_spec)
    grid_spec = pltpu.PrefetchScalarGridSpec(
        num_scalar_prefetch=1,
        grid=(heads // pack, count),
        in_specs=[query_spec] + [kv_spec] * blocks + ([] if start else [sum_spec, top_spec, query_spec]),
        out_specs=out_specs,
        scratch_shapes=scratch,
    )
    pairs = heads * 5 * count // 2
    return pl.pallas_call(
        functools.partial(attend_kernel, blocks=blocks, pack=pack, at=at, start=start, end=end),
        out_shape=outs,
        grid_spec=grid_spec,
        compiler_params=params(),
        cost_estimate=cost(
            pairs * 8 * tok * tok * AH, blocks * 4 * tok * features, pairs * tok * tok
        ),
        name="attend",
    )(ids, queries, *kvs, *(() if start else (*carry, fast)))


def answer_kernel(query_ref, weight_ref, gain_ref, out_ref):
    query = query_ref[0].astype(F32)
    normed = (query * rms_inverse(query)).astype(BF16)
    first = dot_nn(normed, weight_ref[0])
    third = dot_nn(normed, weight_ref[1])
    hidden = (first * sigmoid(first) * third).astype(BF16)
    answer = dot_nn(hidden, weight_ref[2])
    out_ref[0] = answer * rms_inverse(answer) * gain_ref[...]


def answer(queries, weights, gain):
    two, tok, width = queries.shape
    block = pl.BlockSpec((1, tok, width), lambda w: (w, 0, 0))
    return pl.pallas_call(
        answer_kernel,
        out_shape=jax.ShapeDtypeStruct(queries.shape, F32),
        grid=(two,),
        in_specs=[
            block,
            pl.BlockSpec(weights.shape, lambda w: (0, 0, 0)),
            pl.BlockSpec((1, width), lambda w: (0, 0)),
        ],
        out_specs=block,
        compiler_params=params(),
        cost_estimate=cost(two * 6 * tok * width * width, 10 * tok * width),
        name="answer",
    )(queries, weights, gain)


def project_kernel(which_ref, own_ref, got_ref, own_weight_ref, got_weight_ref, out_ref):
    total = dot_nn(own_ref[0], own_weight_ref[...]) + dot_nn(got_ref[0], got_weight_ref[...])
    out_ref[...] = total.astype(BF16)


def project(which, own, got, weight):
    count, depth = own.shape[1:]
    columns = weight.shape[1]
    wide = 512
    rows = pl.BlockSpec((1, count, depth), lambda i, s: (0, 0, 0))
    grid_spec = pltpu.PrefetchScalarGridSpec(
        num_scalar_prefetch=1,
        grid=(columns // wide,),
        in_specs=[
            rows,
            rows,
            pl.BlockSpec((depth, wide), lambda i, s: (s[0], i)),
            pl.BlockSpec((depth, wide), lambda i, s: (1 - s[0], i)),
        ],
        out_specs=pl.BlockSpec((count, wide), lambda i, s: (0, i)),
    )
    return pl.pallas_call(
        project_kernel,
        out_shape=jax.ShapeDtypeStruct((count, columns), BF16),
        grid_spec=grid_spec,
        compiler_params=params(),
        cost_estimate=cost(4 * count * depth * columns, 4 * depth * columns),
        name="project",
    )(which[None].astype(jnp.int32), own, got, weight, weight)


def shards(queries, keys, values, token_rates, fast_init, out_gain, out_weight):
    spans, tok, features = queries.shape
    width = fast_init.shape[2]
    position = lax.axis_index("ctx")
    around = lax.axis_size("ctx")
    upper = around // 2
    core = position % 2
    side = (position // 2) % 2
    far = position // upper
    here = side == 0
    core_one = core[None].astype(jnp.int32)

    def keep(array):
        return jnp.where(here, array[..., :width], array[..., width:])

    def give(array):
        return jnp.where(here, array[..., width:], array[..., :width])

    def column(rates):
        return jnp.broadcast_to(rates[:, None], (tok, 128))

    def added(left, right):
        return (left.astype(F32) + right.astype(F32)).astype(BF16)

    own_place = 2 * side + core
    got_place = 2 * (1 - side) + core
    own_pair = 2 * side + 1 - core
    got_pair = 2 * (1 - side) + 1 - core
    places = jnp.stack([own_place, got_place, own_pair, got_pair]).astype(jnp.int32)

    def ids(span, *bases):
        mine = span * around + far * upper + places[:2]
        return jnp.concatenate([mine] + [base + places for base in bases]).astype(jnp.int32)

    def total_over_heads(product):
        return lax.psum_scatter(product, "head", scatter_dimension=0, tiled=True)

    kv_away0, kv_own0 = split(side, keys, values, 0)
    kv_got0 = swapped(kv_away0, 2)
    far_own0 = swapped(kv_own0, upper)
    pair_own0 = swapped(kv_own0, 1)
    rates_away = jnp.where(here, token_rates[..., 1], token_rates[..., 0])
    rates_got = swapped(rates_away, 2)
    rates_own = jnp.where(here, token_rates[..., 0], token_rates[..., 1])
    weights0 = jnp.where(here, fast_init[:, 0], fast_init[:, 1]).astype(BF16)
    gain = keep(out_gain[None, :])
    partial0 = grads_first(kv_own0, column(rates_own[0]), weights0)

    query_got0 = swapped(after(give(queries[0]), kv_got0, partial0), 2)
    far_got0 = swapped(after(kv_got0, far_own0, partial0), upper)
    pair_got0 = swapped(after(kv_got0, partial0), 1)
    kv_away1, kv_own1 = split(after(side, partial0), keys, values, 1)
    kv_got1 = swapped(after(kv_away1, query_got0), 2)
    keep0, give0 = grads_second(
        after(core_one, partial0, kv_own1, query_got0), kv_got0, column(rates_got[0]), weights0, partial0
    )
    chip0 = added(keep0, swapped(give0, 1))
    query0 = jnp.stack([keep(queries[0]), query_got0])
    near0 = attend(
        after(ids(0, far * upper), keep0), query0, [kv_own0, kv_got0, pair_own0, pair_got0]
    )
    pair_far_own0 = swapped(far_own0, 1)
    pair_far_got0 = swapped(after(far_got0, near0[1]), 1)
    fast0 = answer(after(query0, near0[1], chip0), weights0, gain)
    other0 = swapped(after(chip0, far_got0, near0[1]), upper)
    fars0 = [far_own0, far_got0, pair_far_own0, pair_far_got0]
    late = jnp.where(far == 0, NOWHERE, 0)
    ids0 = ids(0, late)
    mixed_got0 = attend(after(ids0, fast0, kv_got1), query0, fars0, near0, fast0, 1)
    returned0 = swapped(mixed_got0, 2)
    far_own1 = raised(after(kv_own1, other0, mixed_got0), upper)
    total0 = added(chip0, after(other0, mixed_got0))
    pair_total0 = swapped(total0, 1)
    mixed_own0 = attend(after(ids0, mixed_got0, total0), query0, fars0, near0, fast0, 0)
    product0 = project(side, mixed_own0, returned0, out_weight)
    layer0 = total_over_heads(after(product0, far_own1))

    query_got1 = swapped(after(give(queries[1]), kv_got1, returned0), 2)
    ortho0, half0, weights1 = muon(after(core, product0), total0, pair_total0, fast_init, side)
    far_got1 = raised(after(kv_got1, far_own1, product0), upper)
    pair_own1 = swapped(after(kv_own1, product0), 1)
    pair_got1 = swapped(after(kv_got1, product0), 1)
    pair_far_own1 = swapped(after(far_own1, half0), 1)
    query1 = jnp.stack([keep(queries[1]), query_got1])
    fast1 = answer(after(query1, half0), weights1, gain)
    away0 = swapped(after(half0, query_got1, fast1), 2)
    near1 = attend(
        after(ids(1, around + far * upper), fast1),
        query1,
        [kv_own1, kv_got1, pair_own1, pair_got1],
    )
    pair_far_got1 = swapped(after(far_got1, fast1), 1)
    fars1 = [far_own1, far_got1, pair_far_own1, pair_far_got1]
    early = jnp.where(far == 0, around - upper, NOWHERE)
    late = jnp.where(far == 0, NOWHERE, around)
    ids1 = ids(1, early, late)
    mixed_got1 = attend(after(ids1, near1[1]), query1, fars0 + fars1, near1, fast1, 1)
    returned1 = swapped(mixed_got1, 2)
    mixed_own1 = attend(after(ids1, mixed_got1), query1, fars0 + fars1, near1, fast1, 0)
    product1 = project(side, mixed_own1, returned1, out_weight)
    keep1, give1 = grads_both(
        after(core_one, product1),
        kv_own1,
        column(rates_own[1]),
        kv_got1,
        column(rates_got[1]),
        weights1,
    )
    chip1 = added(keep1, swapped(give1, 1))
    other1 = swapped(chip1, upper)
    total1 = added(chip1, other1)
    pair_total1 = swapped(total1, 1)
    pair_away0 = swapped(after(away0, product1), 1)
    layer1 = total_over_heads(product1)

    ortho1, half1 = muon(after(core, product1), total1, pair_total1)
    away1 = swapped(half1, 2)
    state = finish(core, side, fast_init, [ortho0, ortho1])
    pair_away1 = swapped(after(away1, state), 1)
    state = finish(
        core, side, fast_init, [away0, pair_away0, away1, pair_away1], after(state, away1)
    )
    layer_out = jnp.stack([layer0, layer1], 0)
    return (layer_out, state)


def shifted(block, axis, distance):
    devices = range(lax.axis_size(axis))
    route = [((i - distance) % len(devices), i) for i in devices]
    return lax.ppermute(block, axis, route)


def head_norm(inputs):
    return inputs / jnp.sqrt(jnp.mean(inputs * inputs, axis=-1, keepdims=True) + 1e-06)


def renormed(previous, fresh):
    target = jnp.sqrt(jnp.mean(previous * previous, axis=-1, keepdims=True) + 1e-06)
    actual = jnp.sqrt(jnp.mean(fresh * fresh, axis=-1, keepdims=True) + 1e-06)
    return fresh * target / actual


def newton_turn(ortho, gram):
    gram_bf = gram.astype(jnp.bfloat16)
    square = jnp.einsum("mhij,mhjk->mhik", gram_bf, gram_bf, preferred_element_type=jnp.float32)
    poly = (coef_b * gram_bf.astype(jnp.float32) + coef_c * square).astype(jnp.bfloat16)
    moved = jnp.einsum("rmhi,mhij->rmhj", ortho, poly, preferred_element_type=jnp.float32)
    return (coef_a * ortho.astype(jnp.float32) + moved).astype(jnp.bfloat16)


def fix_wrapped(received, distance, position):
    rolled = jnp.concatenate([jnp.zeros_like(received[:1]), received[:-1]], 0)
    return jnp.where(position < distance, rolled, received)


def shards_any(queries, keys, values, token_rates, fast_init, out_gain, out_weight):
    spans, tok, features = queries.shape
    per_dev = fast_init.shape[1]
    width = fast_init.shape[2]
    att_heads = features // AH
    position = lax.axis_index("ctx")
    far_keys = []
    far_values = []
    carried = (keys, values)
    for distance in (1, 2, 3, 4):
        carried = shifted((carried[0], carried[1]), "ctx", 1)
        far_keys.insert(0, fix_wrapped(carried[0], distance, position))
        far_values.insert(0, fix_wrapped(carried[1], distance, position))
    window_keys = jnp.concatenate(far_keys + [keys], 1)
    window_values = jnp.concatenate(far_values + [values], 1)
    scale = AH ** (-0.5)
    query_pos = jnp.arange(tok, dtype=jnp.int32)[:, None]
    key_pos = jnp.arange(5 * tok, dtype=jnp.int32)[None, :]
    distance_pos = query_pos + 4 * tok - key_pos
    in_window = (distance_pos >= 0) & (distance_pos < 4 * tok)
    key_shard = 4 - key_pos // tok
    gain = out_gain.reshape(per_dev, width)
    state = fast_init
    mixed_all = []
    for span in range(spans):
        valid = in_window
        if span == 0:
            valid = valid & jnp.logical_not(position < key_shard)
        query_heads = queries[span].reshape(tok, att_heads, AH)
        key_heads = window_keys[span].reshape(5 * tok, att_heads, AH)
        value_heads = window_values[span].reshape(5 * tok, att_heads, AH)
        scores = (
            jnp.einsum("qnd,knd->nqk", query_heads, key_heads, preferred_element_type=jnp.float32)
            * scale
        )
        scores = jnp.where(valid[None], scores, -1e30)
        largest = jnp.max(scores, axis=-1, keepdims=True)
        expon = jnp.exp(scores - largest)
        probs = (expon / jnp.sum(expon, axis=-1, keepdims=True)).astype(jnp.bfloat16)
        attn = jnp.einsum(
            "nqk,knd->qnd", probs, value_heads, preferred_element_type=jnp.float32
        ).reshape(tok, features)
        query_norm = head_norm(
            queries[span].reshape(tok, per_dev, width).astype(jnp.float32)
        ).astype(jnp.bfloat16)
        key_norm = head_norm(keys[span].reshape(tok, per_dev, width).astype(jnp.float32)).astype(
            jnp.bfloat16
        )
        value_own = values[span].reshape(tok, per_dev, width)
        weights_bf = state.astype(jnp.bfloat16)
        q_first = jnp.einsum(
            "shd,hde->she", query_norm, weights_bf[0], preferred_element_type=jnp.float32
        )
        q_third = jnp.einsum(
            "shd,hde->she", query_norm, weights_bf[1], preferred_element_type=jnp.float32
        )
        query_hidden = (q_first * jax.nn.sigmoid(q_first) * q_third).astype(jnp.bfloat16)
        fast_out = jnp.einsum(
            "she,hed->shd", query_hidden, weights_bf[2], preferred_element_type=jnp.float32
        )
        first = jnp.einsum(
            "shd,hde->she", key_norm, weights_bf[0], preferred_element_type=jnp.float32
        )
        third = jnp.einsum(
            "shd,hde->she", key_norm, weights_bf[1], preferred_element_type=jnp.float32
        )
        sigma = jax.nn.sigmoid(first)
        key_hidden = (first * sigma * third).astype(jnp.bfloat16)
        pull = (-token_rates[span][:, :, None] * value_own.astype(jnp.float32)).astype(jnp.bfloat16)
        back = jnp.einsum("shd,hed->she", pull, weights_bf[2], preferred_element_type=jnp.float32)
        d_first = (back * third * sigma * (1.0 + first * (1.0 - sigma))).astype(jnp.bfloat16)
        d_third = (back * first * sigma).astype(jnp.bfloat16)
        grad_first = jnp.einsum(
            "shr,she->rhe", key_norm, d_first, preferred_element_type=jnp.float32
        )
        grad_third = jnp.einsum(
            "shr,she->rhe", key_norm, d_third, preferred_element_type=jnp.float32
        )
        grad_down = jnp.einsum("shr,shd->rhd", key_hidden, pull, preferred_element_type=jnp.float32)
        grad_rows = lax.psum_scatter(
            jnp.stack([grad_first, grad_third, grad_down], 1).astype(jnp.bfloat16),
            "ctx",
            scatter_dimension=0,
            tiled=True,
        ).astype(jnp.float32)
        squares = lax.psum(jnp.sum(grad_rows * grad_rows, axis=(0, 3)), "ctx")
        ortho_rows = (grad_rows * lax.rsqrt(squares + 1e-06)[None, :, :, None]).astype(jnp.bfloat16)
        ortho = lax.all_gather(ortho_rows, "ctx", axis=0, tiled=True)
        for turn in range(NS_ITERS):
            gram = jnp.einsum("rmhi,rmhj->mhij", ortho, ortho, preferred_element_type=jnp.float32)
            ortho = newton_turn(ortho, gram)
        ortho_mats = jnp.transpose(ortho, (1, 2, 0, 3)).astype(jnp.float32)
        state = renormed(state, state - ortho_mats)
        normed = head_norm(fast_out) * gain
        mixed_all.append((normed.reshape(tok, features) + attn).astype(jnp.bfloat16))
    combined = jnp.stack(mixed_all, 0)
    product = jnp.einsum("ctd,de->tce", combined, out_weight, preferred_element_type=jnp.float32)
    summed = lax.psum_scatter(
        product.astype(jnp.bfloat16), "head", scatter_dimension=0, tiled=True
    ).astype(jnp.float32)
    layer_out = jnp.transpose(summed, (1, 0, 2)).astype(jnp.bfloat16)
    return (layer_out, state)


def plan(queries, keys, values, token_rates, fast_init, out_gain, out_weight):
    halved = lax.axis_size("ctx") == 2 * BACK and fast_init.shape[1] == 2 and queries.shape[0] == 2
    chosen = shards if halved else shards_any
    return chosen(queries, keys, values, token_rates, fast_init, out_gain, out_weight)


def solution(mesh):
    placed = (
        P(None, "ctx", "head"),
        P(None, "ctx", "head"),
        P(None, "ctx", "head"),
        P(None, "ctx", "head"),
        P(None, "head", None, None),
        P("head"),
        P("head", None),
    )
    return jax.shard_map(
        plan,
        mesh=mesh,
        in_specs=placed,
        out_specs=(P(None, ("ctx", "head"), None), P(None, "head", None, None)),
        check_vma=False,
    )
```
